256 devices in a mesh: section: 2 (over core), dp: 16 (over x, y), tensor: 8 (over z).
Axes of the slice: x: 4, y: 4, z: 8, core: 2. Of those that a mesh axis runs over, the one named last changes fastest.
Arguments:
- hidden_states: bfloat16 [2, 4096, 8192], P('section', 'dp', 'tensor'), may hold values from -6 to 6
- base_weight: bfloat16 [2, 8192, 8192], P('section', 'tensor', 'dp'), may hold values from -0.0625 to 0.0625
- shrink_weight: bfloat16 [2, 1024, 16, 8192], P('section', 'dp', None, 'tensor'), may hold values from -0.0625 to 0.0625
- expand_weight: bfloat16 [2, 1024, 16, 8192], P('section', 'dp', None, 'tensor'), may hold values from -1.5 to 1.5
- owner_ids: int32 [2, 4096, 1], P('section', 'dp'), may hold values from 0 to 15; in each aligned block of 256 rows (0 to 255, 256 to 511, ..., all dimensions but the last counted through in order) at most 32 rows name the same one
- adapter_slots: int32 [2, 4096], P('section', 'dp'), may hold values from 0 to 63
Outputs:
- carried: bfloat16 [2, 4096, 8192], P('section', 'dp', 'tensor')
The draws below stay inside these ranges and needn't reach their ends.
Inputs may be any that keep to these rules, and one draw needn't show every extreme that they name: `owner_ids`: within each aligned block of 256 rows (the rows of one device), no owner is named by more than 32 rows, and one owner is named by exactly 32 rows in some block.
All inputs are finite; a program needn't handle non-finite values.
Results may differ from the reference program's by a relative error of at most 0.017.
Values may be sent and summed in bfloat16 or wider, within the bound.
A program may use at most 128 MiB of HBM per device.

```python
import math
import jax
import jax.numpy as jnp
import numpy as np
from jax import lax

D = 8192
RANK = 16
ADAPT_DEV = 64
TOK_DEV = 256
SECTIONS = 2
OWNERS = 16
TOKENS = 4096
ADAPTERS = 1024
CAP = 32
N_TENSOR = 8


def set_ends(drawn, rng, smallest, largest):
    shape = drawn.shape
    index_at = [jax.random.randint(jax.random.fold_in(rng, axis), (), 0, shape[axis]) for axis in range(len(shape))]
    drawn = drawn.at[tuple(index_at)].set(smallest)
    longest = shape.index(max(shape))
    index_at[longest] = (index_at[longest] + 1) % shape[longest]
    return drawn.at[tuple(index_at)].set(largest)


def level_of(own_key, extent, cuts, smallest, top_value):
    def one(axis_at, parts):
        steps = jax.random.uniform(jax.random.fold_in(jax.random.fold_in(own_key, 6), axis_at), (parts,), jnp.float32, smallest / len(cuts), top_value / len(cuts))
        return jnp.repeat(jnp.exp(steps), extent[axis_at] // parts).reshape((-1,) + (1,) * (len(extent) - axis_at - 1))

    loudness = one(*cuts[0])
    for cut in cuts[1:]:
        loudness = loudness * one(*cut)
    return loudness


def rank_bounds(count, skew):
    portions = [(1 << 20) // math.isqrt(grade ** skew) + 1 for grade in range(1, count + 1)]
    width = 1 + sum(portions) // (1 << 30)
    return np.cumsum(np.array([max(1, weight // width) for weight in portions]))


def ranked(own_key, extent, number_of, lean):
    grid = rank_bounds(number_of, lean)
    ticket = jax.random.randint(jax.random.fold_in(own_key, 1), extent, 0, int(grid[number_of - 1]))
    grade = jnp.searchsorted(jnp.asarray(grid, jnp.int32), ticket, side="right")
    return jax.random.permutation(jax.random.fold_in(own_key, 2), number_of)[grade].astype(jnp.int32)


def assign_block(rng, own, number, rows, number_of, top, most, skew):
    ranking = jax.random.permutation(rng, number_of)
    crowded, ordinary = portions_of(number_of, rows * top, most, skew, True), portions_of(number_of, rows * top, most, skew, False)
    places = jnp.arange(number_of)

    def named(sizes, offset_by):
        used = int((sizes > 0).sum())
        fixed = max(1, used // 4)
        shifted = fixed + (places - fixed + offset_by * (used - fixed)) % max(1, number_of - fixed)
        return jnp.zeros((number_of,), jnp.int32).at[ranking[jnp.where(places < fixed, places, shifted)]].set(jnp.asarray(sizes, jnp.int32))

    sizes = jnp.where(number % 4 == 0, named(crowded, number // 4), named(ordinary, number - number // 4 - 1))
    mixed = jax.random.permutation(jax.random.fold_in(own, 3), number_of)
    source_of, taker = mixed[0:number_of // 2 * 2:2], mixed[1:number_of // 2 * 2:2]
    margin = jnp.minimum(sizes[source_of] - 1, most - sizes[taker]) // 2
    margin = jnp.where((source_of == ranking[0]) | (taker == ranking[0]) | (sizes[taker] == 0), 0, jnp.maximum(margin, 0))
    shifted = jax.random.randint(jax.random.fold_in(own, 4), (number_of // 2,), 0, 1 << 20) % (margin + 1)
    sizes = sizes.at[source_of].add(-shifted).at[taker].add(shifted)
    members = jnp.searchsorted(jnp.cumsum(sizes), jnp.arange(rows * top), side="right").astype(jnp.int32)
    grid = members.reshape(top, rows).T
    grid = grid[jax.random.permutation(jax.random.fold_in(own, 1), rows)]
    offset_by = jax.random.randint(jax.random.fold_in(own, 2), (rows, 1), 0, top)
    return jnp.take_along_axis(grid, (jnp.arange(top)[None, :] + offset_by) % top, axis=1)


def portions_of(count, total, reach, skew, full):
    weights = [(1 << 20) // math.isqrt(rank ** skew) + 1 for rank in range(1, count + 1)]
    largest = reach if full else min(reach, max(-(-total // count), total * weights[0] // sum(weights)))
    least = 1 if total - largest >= count - 1 else 0
    counts, surplus = [largest] + [least] * (count - 1), total - largest - least * (count - 1)
    while surplus > 0:
        free = [i for i in range(1, count) if counts[i] < largest] or [i for i in range(1, count) if counts[i] < reach]
        whole, left = sum([weights[i] for i in free]), surplus
        for i in free:
            more = min(reach - counts[i], max(1, left * weights[i] // whole), surplus)
            counts[i] = counts[i] + more
            surplus = surplus - more
    return np.array(counts)


def centred(own_key, shape, scale, reach, shards=(), held_as=jnp.bfloat16):
    factor_of = level_of(own_key, shape, shards, -0.22, 0.18) if shards else 1.0
    result = jax.random.normal(own_key, shape, jnp.float32) * scale * factor_of
    return jnp.minimum(jnp.maximum(result, -reach), reach).astype(held_as)


def setup_inputs(seed: int = 0) -> dict:
    streams_of = jax.random.split(jax.random.key(seed), 7)
    hidden_states = centred(streams_of[0], (SECTIONS, TOKENS, D), 1.0, 6.0, ((0, 2), (1, 16), (2, 8)))
    base_weight = centred(streams_of[1], (SECTIONS, D, D), D ** -0.5, 0.0625, ((0, 2), (1, 8), (2, 16)))
    shrink_weight = centred(streams_of[2], (SECTIONS, ADAPTERS, RANK, D), D ** -0.5, 0.0625, ((0, 2), (1, 16), (3, 8)))
    expand_weight = centred(streams_of[3], (SECTIONS, ADAPTERS, RANK, D), RANK ** -0.5, 1.5, ((0, 2), (1, 16), (3, 8)))
    owner_ids_keys = jax.random.split(jax.random.fold_in(streams_of[4], 1), SECTIONS * TOKENS // TOK_DEV)
    owner_ids_turns = jax.random.permutation(jax.random.fold_in(streams_of[4], 3), SECTIONS * TOKENS // TOK_DEV)
    owner_ids = jax.vmap(lambda own, number: assign_block(jax.random.fold_in(streams_of[4], 2), own, number, TOK_DEV, OWNERS, 1, CAP, 2))(owner_ids_keys, owner_ids_turns).reshape((SECTIONS, TOKENS, 1))
    adapter_slots = set_ends(ranked(streams_of[5], (SECTIONS, TOKENS), ADAPT_DEV, 2), jax.random.fold_in(streams_of[5], 3), 0, ADAPT_DEV - 1).astype(jnp.int32)
    return dict(hidden_states=hidden_states, base_weight=base_weight, shrink_weight=shrink_weight, expand_weight=expand_weight, owner_ids=owner_ids, adapter_slots=adapter_slots)


def base_product(states, weight):
    slice_width = D // N_TENSOR
    pieces = states.reshape(TOKENS, N_TENSOR, slice_width).transpose(1, 0, 2)
    blocks = weight.reshape(N_TENSOR, slice_width, D)

    def add_part(running, operands):
        partial_value = jnp.dot(operands[0], operands[1], preferred_element_type=jnp.float32)
        rounded = lax.optimization_barrier(partial_value.astype(jnp.bfloat16))
        return running + rounded.astype(jnp.float32), None

    running, _ = lax.scan(add_part, jnp.zeros((TOKENS, D), jnp.float32), (pieces, blocks))
    return running


def adapter_output(states, shrink, expand, adapters):
    block_rows = math.gcd(TOKENS, 512)
    block_count = TOKENS // block_rows

    def one_block(block_index):
        first_row = block_index * block_rows
        row_values = lax.dynamic_slice_in_dim(states, first_row, block_rows, 0).astype(jnp.float32)
        chosen = lax.dynamic_slice_in_dim(adapters, first_row, block_rows, 0)
        down_rows = shrink[chosen].astype(jnp.float32)
        shrunk = jnp.einsum("td,trd->tr", row_values, down_rows).astype(jnp.bfloat16)
        shrunk = lax.optimization_barrier(shrunk).astype(jnp.float32)
        up_rows = expand[chosen].astype(jnp.float32)
        return jnp.einsum("tr,trd->td", shrunk, up_rows).astype(jnp.bfloat16)

    stacked = lax.map(one_block, jnp.arange(block_count, dtype=jnp.int32))
    return stacked.reshape(TOKENS, D)


def reference(hidden_states, base_weight, shrink_weight, expand_weight, owner_ids, adapter_slots):
    results = []
    for section_index in range(SECTIONS):
        states = hidden_states[section_index]
        adapters = (owner_ids[section_index, :, 0] * ADAPT_DEV + adapter_slots[section_index]).astype(jnp.int32)
        base_term = base_product(states, base_weight[section_index])
        low_rank = adapter_output(states, shrink_weight[section_index], expand_weight[section_index], adapters)
        layer_out = states.astype(jnp.float32) + base_term + low_rank.astype(jnp.float32)
        results.append(layer_out.astype(jnp.bfloat16))
    layered = jnp.stack(results)
    return jnp.roll(layered, 1, axis=0)
```

```python
import functools

import jax
import jax.numpy as jnp
from jax import lax
from jax.experimental import pallas as pl
from jax.experimental.pallas import tpu as pltpu
from jax.sharding import PartitionSpec as P

MESH = pl.DeviceIdType.MESH
NX, NY, NZ = 4, 4, 8
ROWS, WIDTH, COLS = 256, 1024, 512
OWNERS, CAP, SLOTS, RANK = 16, 32, 64, 16
NQ = 4
CW = COLS // NQ
STARTS = (0, 0, 4, 6)
ROUNDS = 8 + max(STARTS)
FWD_W = {2: 1, 3: 4}
E1_AT, E2_AT = 7, 9
BF, F32 = jnp.bfloat16, jnp.float32


def remote(src, dst, send, recv, device):
    return pltpu.make_async_remote_copy(
        src_ref=src, dst_ref=dst, send_sem=send, recv_sem=recv, device_id=device, device_id_type=MESH
    )


def dot(a, b, ca, cb):
    return lax.dot_general(a, b, (((ca,), (cb,)), ((), ())), preferred_element_type=F32)


def arrivals(owner, upper):
    hits = lax.broadcasted_iota(jnp.int32, (OWNERS, ROWS), 0) == owner
    count = dot(hits.astype(BF), upper, 1, 0)
    return (jnp.sum(jnp.where(hits, count, 0.0), axis=0, keepdims=True) - 1.0).astype(jnp.int32)


def kernel(
    x_hbm, w_hbm, shrink_hbm, expand_hbm, ids_hbm, out_ref,
    xg, wg, idg, rs, bt, xp, idp, aout, sout, ain, sin, shrink, expand, pin, spread, low, lin,
    loc_sem, x_send, x_recv, id_send, id_recv, w_send, w_recv, p_send, p_recv, f_send, f_recv,
    g_send, g_recv, z_send, z_recv, r_send, r_recv, b_send, b_recv, rs_send, rs_recv,
):
    s = lax.axis_index("section")
    dp = lax.axis_index("dp")
    z = lax.axis_index("tensor")
    x, y = dp // NY, dp % NY
    other = 1 - s
    half = y // 2
    here = lambda xx, yy, zz: (s, xx * NY + yy, zz)
    there = lambda xx, yy, zz: (other, xx * NY + yy, zz)
    z_flip = z + 1 - 2 * (z % 2)

    def local(src, dst, i):
        return pltpu.make_async_copy(src, dst, loc_sem.at[i])

    load_x = local(x_hbm, xg.at[y], 0)
    load_id = local(ids_hbm, idg.at[y], 1)
    load_w = [local(w_hbm.at[:, pl.ds(q * CW, CW)], wg.at[x, q], 4 + q) for q in range(NQ)]
    load_shrink = local(shrink_hbm, shrink, 2)
    load_expand = local(expand_hbm, expand, 3)
    load_x.start()
    load_id.start()
    for q in range(NQ):
        load_w[q].start()
    load_shrink.start()
    load_expand.start()

    barrier = pltpu.get_barrier_semaphore()
    peers = [here(x, (y + d) % NY, z) for d in range(1, NY)]
    peers += [here((x + d) % NX, y, z) for d in range(1, NX)]
    peers += [here(x, y, (z + d) % NZ) for d in range(1, NZ)]
    peers += [there(xx, yy, z) for xx in range(NX) for yy in range(NY)]
    peers += [there(x, yy, z_flip) for yy in range(NY)]
    for peer in peers:
        pl.semaphore_signal(barrier, inc=1, device_id=peer, device_id_type=MESH)
    pl.semaphore_wait(barrier, len(peers))

    started = []

    def start(copy):
        copy.start()
        started.append(copy)

    y_up, y_down, y_far = (y + 1) % NY, (y + NY - 1) % NY, (y + 2) % NY
    x_up, x_down, x_far = (x + 1) % NX, (x + NX - 1) % NX, (x + 2) % NX

    def gather(buf, slots, send, recv, up, down):
        mine, below, above, far = slots
        full_up = remote(buf(mine, None), buf(mine, None), send(0), recv(0), up)
        full_down = remote(buf(mine, None), buf(mine, None), send(1), recv(1), down)
        got_below = remote(buf(below, None), buf(below, None), send(0), recv(0), up)
        got_above = remote(buf(above, None), buf(above, None), send(1), recv(1), down)
        pass_up = remote(buf(below, 0), buf(below, 0), send(2), recv(2), up)
        pass_down = remote(buf(above, 1), buf(above, 1), send(3), recv(3), down)
        got_far0 = remote(buf(far, 0), buf(far, 0), send(2), recv(2), up)
        got_far1 = remote(buf(far, 1), buf(far, 1), send(3), recv(3), down)

        def first():
            start(full_up)
            start(full_down)

        def forward():
            got_below.wait_recv()
            pass_up.start()
            got_above.wait_recv()
            pass_down.start()

        def finish():
            got_far0.wait_recv()
            got_far1.wait_recv()

        def drain():
            pass_up.wait_send()
            pass_down.wait_send()

        return first, forward, finish, drain

    def x_buf(slot, part):
        if part is None:
            return xg.at[slot]
        return xg.at[slot, pl.ds(part * (ROWS // 2), ROWS // 2), :]

    def w_buf(q):
        def buf(slot, part):
            if part is None:
                return wg.at[slot, q]
            return wg.at[slot, q, pl.ds(part * (WIDTH // 2), WIDTH // 2), :]

        return buf

    gx = gather(
        x_buf, (y, y_down, y_up, y_far), lambda i: x_send.at[i], lambda i: x_recv.at[i],
        here(x, y_up, z), here(x, y_down, z),
    )
    gw = [
        gather(
            w_buf(q), (x, x_down, x_up, x_far), lambda i, q=q: w_send.at[q, i], lambda i, q=q: w_recv.at[q, i],
            here(x_up, y, z), here(x_down, y, z),
        )
        for q in range(NQ)
    ]

    load_x.wait()
    gx[0]()
    load_id.wait()
    for d in range(1, NY):
        start(remote(idg.at[y], idg.at[y], id_send.at[d - 1], id_recv.at[d - 1], here(x, (y + d) % NY, z)))
    for q in range(NQ):
        load_w[q].wait()
        gw[q][0]()
    partner = there(x, y, z)
    start(remote(xg.at[y], xp, p_send.at[0], p_recv.at[0], partner))
    start(remote(idg.at[y], idp, p_send.at[1], p_recv.at[1], partner))

    gx[1]()
    gw[0][1]()
    for d in range(1, NY):
        src_y = (y + NY - d) % NY
        remote(idg.at[src_y], idg.at[src_y], id_send.at[d - 1], id_recv.at[d - 1], partner).wait_recv()
    gx[2]()

    upper = (
        lax.broadcasted_iota(jnp.int32, (ROWS, ROWS), 0) <= lax.broadcasted_iota(jnp.int32, (ROWS, ROWS), 1)
    ).astype(BF)
    codes, slot_rows = [], []
    for yb in range(NY):
        owner = idg[yb, 0:1, :]
        code = (owner >> 2) * (NY * CAP) + yb * CAP + arrivals(owner, upper)
        codes.append(jnp.where((owner & 3) == y, code, -1))
        slot_rows.append(idg[yb, 1:2, :])
    rows_of_x = NY * CAP
    for yb in range(NY):
        pick = (lax.broadcasted_iota(jnp.int32, (NX * rows_of_x, ROWS), 0) == codes[yb]).astype(BF)
        sub = jnp.concatenate(
            [pick[xx * rows_of_x + yb * CAP : xx * rows_of_x + (yb + 1) * CAP] for xx in range(NX)], axis=0
        )
        rows = dot(sub, xg[yb], 1, 0).astype(BF)
        for xx in range(NX):
            aout[xx, yb * CAP : (yb + 1) * CAP, :] = rows[xx * CAP : (xx + 1) * CAP]
        slot_block = jnp.broadcast_to(slot_rows[yb].astype(F32).astype(BF), (8, ROWS))
        chosen = dot(slot_block, pick, 1, 1)
        for xx in range(NX):
            part = chosen[:, xx * rows_of_x : (xx + 1) * rows_of_x]
            if yb == 0:
                sout[xx] = part
            else:
                sout[xx] = sout[xx] + part
    for d in range(1, NX):
        to = (x + d) % NX
        start(remote(aout.at[to], ain.at[x], f_send.at[d - 1], f_recv.at[d - 1], here(to, y, z)))
        start(remote(sout.at[to], sin.at[x], g_send.at[d - 1], g_recv.at[d - 1], here(to, y, z)))
    ain[x] = aout[x]
    sin[x] = sout[x]

    gw[0][2]()
    gw[1][1]()
    gw[1][2]()

    def rs_parts(q, direction, t):
        if direction == 0:
            block = lax.rem(z - 1 - t + 2 * NZ, NZ)
            to = here(x, y, (z + 1) % NZ)
        else:
            block = lax.rem(z + 1 + t, NZ)
            to = here(x, y, (z + NZ - 1) % NZ)
        aligned = 1 - (block + half) % 2
        off = aligned * direction + (1 - aligned) * (3 - direction)
        return block, lax.rem(y + off, NY), to

    def rs_copy(q, direction, t, to):
        return remote(
            rs.at[direction, q, t], rs.at[direction, q, t + 1],
            rs_send.at[direction, q, t], rs_recv.at[direction, q, t], to,
        )

    def last_copy(q, direction):
        _, row_block, _ = rs_parts(q, direction, NZ - 1)
        dest = there(x, row_block, 2 * (z // 2) + half)
        return remote(
            rs.at[direction, q, NZ - 1], bt.at[y % 2, q], b_send.at[direction, q], b_recv.at[y % 2, q], dest
        )

    def rs_step(q, direction, t):
        block, row_block, to = rs_parts(q, direction, t)
        part = dot(xg[row_block], wg[block // 2, q], 1, 0)

        @pl.when(t == 0)
        def _():
            rs[direction, q, 0] = part.astype(BF)

        @pl.when(t > 0)
        def _():
            rs_copy_in = remote(
                rs.at[direction, q, t], rs.at[direction, q, t],
                rs_send.at[direction, q, t - 1], rs_recv.at[direction, q, t - 1], to,
            )
            rs_copy_in.wait_recv()
            rs[direction, q, t] = (part + rs[direction, q, t].astype(F32)).astype(BF)

        @pl.when(t < NZ - 1)
        def _():
            rs_copy(q, direction, t, to).start()

        @pl.when(t == NZ - 1)
        def _():
            last_copy(q, direction).start()

    def slots_of():
        return jnp.concatenate([sin[xx, 0:1, :] for xx in range(NX)], axis=1).astype(jnp.int32)

    def shrink_part():
        load_shrink.wait()
        for d in range(1, NX):
            src = (x + NX - d) % NX
            remote(ain.at[src], ain.at[src], f_send.at[d - 1], f_recv.at[d - 1], partner).wait_recv()
            remote(sin.at[src], sin.at[src], g_send.at[d - 1], g_recv.at[d - 1], partner).wait_recv()
        slots = slots_of()
        rows = ain[...].reshape(NX * rows_of_x, WIDTH)
        total = jnp.zeros((RANK, NX * rows_of_x), F32)
        group = 16
        for c in range(SLOTS // group):
            projected = dot(shrink[c * group * RANK : (c + 1) * group * RANK, :], rows, 1, 1)
            for k in range(group):
                total = total + jnp.where(
                    slots == c * group + k, projected[k * RANK : (k + 1) * RANK], 0.0
                )
        pin[z] = total.astype(BF)
        for d in range(1, NZ):
            remote(pin.at[z], pin.at[z], z_send.at[d - 1], z_recv.at[d - 1], here(x, y, (z + d) % NZ)).start()

    def return_copy(xx, yb):
        return remote(
            low.at[xx, pl.ds(yb * CAP, CAP), :], lin.at[dp], r_send.at[xx * NY + yb], r_recv.at[dp], there(xx, yb, z)
        )

    def expand_part():
        load_expand.wait()
        for d in range(1, NZ):
            src = (z + NZ - d) % NZ
            remote(pin.at[src], pin.at[src], z_send.at[d - 1], z_recv.at[d - 1], partner).wait_recv()
        slots = slots_of()
        total = pin[0].astype(F32)
        for k in range(1, NZ):
            total = total + pin[k].astype(F32)
        for k in range(SLOTS):
            spread[k * RANK : (k + 1) * RANK, :] = jnp.where(slots == k, total, 0.0).astype(BF)
        for d in range(NX):
            for xx in range(d, d + 1):
                part = dot(spread[:, xx * rows_of_x : (xx + 1) * rows_of_x], expand[...], 0, 0)
                low[xx] = part.astype(BF)
                for yb in range(NY):
                    return_copy(xx, yb).start()

    def round_of(i, carry):
        for q in range(NQ):
            t = i - STARTS[q]
            if STARTS[q] > 0:
                @pl.when(t == 0)
                def _():
                    gw[q][2]()

            @pl.when((t >= 0) & (t < NZ))
            def _():
                for direction in range(2):
                    rs_step(q, direction, t)

        for q, at in FWD_W.items():
            @pl.when(i == at)
            def _():
                gw[q][1]()

        pl.when(i == E1_AT)(shrink_part)
        pl.when(i == E2_AT)(expand_part)
        return carry

    lax.fori_loop(0, ROUNDS, round_of, 0)

    remote(xg.at[y], xp, p_send.at[0], p_recv.at[0], partner).wait_recv()
    remote(idg.at[y], idp, p_send.at[1], p_recv.at[1], partner).wait_recv()
    owner = idp[0:1, :]
    code = owner * CAP + arrivals(owner, upper)
    pick = (lax.broadcasted_iota(jnp.int32, (OWNERS * CAP, ROWS), 0) == code).astype(BF)
    for o in range(OWNERS):
        remote(lin.at[o], lin.at[o], r_send.at[o], r_recv.at[o], partner).wait_recv()
    got = lin[...].reshape(OWNERS * CAP, WIDTH)
    for p in range(2):
        for q in range(NQ):
            remote(bt.at[p, q], bt.at[p, q], b_send.at[0, q], b_recv.at[p, q], partner).wait_recv()
    for c in range(WIDTH // 256):
        cols = slice(c * 256, (c + 1) * 256)
        rows = dot(pick, got[:, cols], 0, 0)
        p, q = (c * 256) // COLS, ((c * 256) % COLS) // CW
        base = jnp.concatenate([bt[p, q + k] for k in range(256 // CW)], axis=1)
        out_ref[:, cols] = (xp[:, cols].astype(F32) + base.astype(F32) + rows).astype(BF)

    for copy in started:
        copy.wait_send()
    gx[3]()
    for q in range(NQ):
        gw[q][3]()
        for direction in range(2):
            for t in range(NZ - 1):
                rs_copy(q, direction, t, partner).wait_send()
            last_copy(q, direction).wait_send()
    for d in range(1, NZ):
        remote(pin.at[z], pin.at[z], z_send.at[d - 1], z_recv.at[d - 1], partner).wait_send()
    for xx in range(NX):
        for yb in range(NY):
            return_copy(xx, yb).wait_send()


def local_part(hidden_states, base_weight, shrink_weight, expand_weight, owner_ids, adapter_slots):
    ids = jnp.concatenate(
        [owner_ids.reshape(1, ROWS), adapter_slots.reshape(1, ROWS), jnp.zeros((6, ROWS), jnp.int32)], axis=0
    )
    dma = pltpu.SemaphoreType.DMA
    any_spec = pl.BlockSpec(memory_space=pl.ANY)
    rows_of_x = NY * CAP
    out = pl.pallas_call(
        kernel,
        out_shape=jax.ShapeDtypeStruct((ROWS, WIDTH), BF),
        in_specs=[any_spec] * 5,
        out_specs=pl.BlockSpec(memory_space=pltpu.VMEM),
        scratch_shapes=[
            pltpu.VMEM((NY, ROWS, WIDTH), BF),
            pltpu.VMEM((NX, NQ, WIDTH, CW), BF),
            pltpu.VMEM((NY, 8, ROWS), jnp.int32),
            pltpu.VMEM((2, NQ, NZ, ROWS, CW), BF),
            pltpu.VMEM((2, NQ, ROWS, CW), BF),
            pltpu.VMEM((ROWS, WIDTH), BF),
            pltpu.VMEM((8, ROWS), jnp.int32),
            pltpu.VMEM((NX, rows_of_x, WIDTH), BF),
            pltpu.VMEM((NX, 8, rows_of_x), F32),
            pltpu.VMEM((NX, rows_of_x, WIDTH), BF),
            pltpu.VMEM((NX, 8, rows_of_x), F32),
            pltpu.VMEM((SLOTS * RANK, WIDTH), BF),
            pltpu.VMEM((SLOTS * RANK, WIDTH), BF),
            pltpu.VMEM((NZ, RANK, NX * rows_of_x), BF),
            pltpu.VMEM((SLOTS * RANK, NX * rows_of_x), BF),
            pltpu.VMEM((NX, rows_of_x, WIDTH), BF),
            pltpu.VMEM((OWNERS, CAP, WIDTH), BF),
            dma((4 + NQ,)),
            dma((4,)), dma((4,)),
            dma((NY - 1,)), dma((NY - 1,)),
            dma((NQ, 4)), dma((NQ, 4)),
            dma((2,)), dma((2,)),
            dma((NX - 1,)), dma((NX - 1,)),
            dma((NX - 1,)), dma((NX - 1,)),
            dma((NZ - 1,)), dma((NZ - 1,)),
            dma((OWNERS,)), dma((OWNERS,)),
            dma((2, NQ)), dma((2, NQ)),
            dma((2, NQ, NZ)), dma((2, NQ, NZ)),
        ],
        compiler_params=pltpu.CompilerParams(
            collective_id=0, has_side_effects=True, vmem_limit_bytes=56 << 20
        ),
    )(
        hidden_states[0],
        base_weight[0],
        shrink_weight[0].reshape(SLOTS * RANK, WIDTH),
        expand_weight[0].reshape(SLOTS * RANK, WIDTH),
        ids,
    )
    return out[None]


def solution(mesh):
    return jax.shard_map(
        local_part,
        mesh=mesh,
        in_specs=(
            P("section", "dp", "tensor"),
            P("section", "tensor", "dp"),
            P("section", "dp", None, "tensor"),
            P("section", "dp", None, "tensor"),
            P("section", "dp", None),
            P("section", "dp"),
        ),
        out_specs=P("section", "dp", "tensor"),
        check_vma=False,
    )
```

```python
import functools

import jax
import jax.numpy as jnp
from jax import lax
from jax.experimental import pallas as pl
from jax.experimental.pallas import tpu as pltpu
from jax.sharding import PartitionSpec as P

MESH = pl.DeviceIdType.MESH
NX, NY, NZ = 4, 4, 8
ROWS, WIDTH, COLS = 256, 1024, 512
OWNERS, CAP, SLOTS, RANK = 16, 32, 64, 16
NQ = 4
CW = COLS // NQ
GROUP = NY * CAP
FLOWS = NQ * NY
STEPS = 3
LAGS = (0, 2, 5, 8, 10)
ROUNDS = FLOWS + LAGS[4]
SEND_W = {2: 2, 3: 6}
PASS_W = {1: 1, 2: 5, 3: 9}
ROUTE_AT = 9
SHRINK_AT = (15, 15, 16, 16)
EXPAND_AT = (19, 19, 20, 20)
PARTS = 4
BF, F32 = jnp.bfloat16, jnp.float32


def remote(src, dst, send, recv, device):
    return pltpu.make_async_remote_copy(
        src_ref=src, dst_ref=dst, send_sem=send, recv_sem=recv, device_id=device, device_id_type=MESH
    )


def dot(a, b, ca, cb):
    return lax.dot_general(a, b, (((ca,), (cb,)), ((), ())), preferred_element_type=F32)


def arrivals(owner, upper):
    hits = lax.broadcasted_iota(jnp.int32, (OWNERS, ROWS), 0) == owner
    count = dot(hits.astype(BF), upper, 1, 0)
    return (jnp.sum(jnp.where(hits, count, 0.0), axis=0, keepdims=True) - 1.0).astype(jnp.int32)


def kernel(
    x_hbm, w_hbm, shrink_hbm, expand_hbm, ids_hbm, out_ref,
    xg, wg, idg, rs, bt, xp, idp, aout, sout, ain, sin, shrink, expand, total, pin, spread, low, lin,
    loc_sem, x_send, x_recv, id_send, id_recv, w_send, w_recv, p_send, p_recv, f_send, f_recv,
    g_send, g_recv, z_send, z_recv, r_send, r_recv, b_send, b_recv, rs_send, rs_recv,
):
    s = lax.axis_index("section")
    dp = lax.axis_index("dp")
    z = lax.axis_index("tensor")
    x, y = dp // NY, dp % NY
    u, v = y, x
    place = lambda uu, vv: vv * NY + uu
    here = lambda uu, vv, zz: (s, place(uu, vv), zz)
    there = lambda uu, vv, zz: (1 - s, place(uu, vv), zz)
    odd = (z + u // 2) % 2
    partner = (1 - s, dp, z)

    def local(src, dst, i):
        return pltpu.make_async_copy(src, dst, loc_sem.at[i])

    block_of = lambda b: xg.at[pl.ds(pl.multiple_of(b * ROWS, ROWS), ROWS), :]
    load_x = local(x_hbm, block_of(u), 0)
    load_id = local(ids_hbm, idg.at[u], 1)
    load_w = [local(w_hbm.at[:, pl.ds(q * CW, CW)], wg.at[v, q], 4 + q) for q in range(NQ)]
    load_shrink = local(shrink_hbm, shrink, 2)
    load_expand = local(expand_hbm, expand, 3)
    load_x.start()
    for q in range(NQ):
        load_w[q].start()
    load_id.start()
    load_shrink.start()
    load_expand.start()

    barrier = pltpu.get_barrier_semaphore()
    peers = [here((u + d) % NY, v, z) for d in range(1, NY)]
    peers += [here(u, (v + d) % NX, z) for d in range(1, NX)]
    peers += [here(u, v, (z + d) % NZ) for d in range(1, NZ)]
    peers += [(1 - s, o, z) for o in range(OWNERS)]
    for peer in peers:
        pl.semaphore_signal(barrier, inc=1, device_id=peer, device_id_type=MESH)
    pl.semaphore_wait(barrier, len(peers))

    started = []

    def start(copy):
        copy.start()
        started.append(copy)

    def gather(buf, slots, send, recv, up, down):
        mine, below, above, far = slots
        sends = [remote(buf(mine, h), buf(mine, h), send(i), recv(i), to) for i, (h, to) in enumerate(
            [(0, up), (1, down), (1, up), (0, down)])]
        arrive = [remote(buf(slot, h), buf(slot, h), send(i), recv(i), up) for i, (slot, h) in enumerate(
            [(below, 0), (above, 1), (below, 1), (above, 0)])]
        pass_up = remote(buf(below, 0), buf(below, 0), send(4), recv(4), up)
        pass_down = remote(buf(above, 1), buf(above, 1), send(5), recv(5), down)
        far_up = remote(buf(far, 0), buf(far, 0), send(4), recv(4), up)
        far_down = remote(buf(far, 1), buf(far, 1), send(5), recv(5), down)

        def first():
            for copy in sends:
                copy.start()

        def forward():
            arrive[0].wait_recv()
            pass_up.start()
            arrive[1].wait_recv()
            pass_down.start()

        def finish_below():
            arrive[2].wait_recv()

        def finish_above():
            arrive[3].wait_recv()

        def finish_far():
            far_up.wait_recv()
            far_down.wait_recv()

        def finish():
            finish_below()
            finish_above()
            finish_far()

        def drain():
            for copy in sends:
                copy.wait_send()
            pass_up.wait_send()
            pass_down.wait_send()

        return first, forward, finish_below, finish_above, finish_far, finish, drain

    u_up, u_down, u_far = (u + 1) % NY, (u + NY - 1) % NY, (u + 2) % NY
    v_up, v_down, v_far = (v + 1) % NX, (v + NX - 1) % NX, (v + 2) % NX
    x_buf = lambda slot, h: xg.at[pl.ds(pl.multiple_of(slot * ROWS + h * (ROWS // 2), ROWS // 2), ROWS // 2), :]
    w_buf = lambda q: lambda slot, h: wg.at[slot, q, pl.ds(h * (WIDTH // 2), WIDTH // 2), :]
    gx = gather(
        x_buf, (u, u_down, u_up, u_far), lambda i: x_send.at[i], lambda i: x_recv.at[i],
        here(u_up, v, z), here(u_down, v, z),
    )
    gw = lambda q: gather(
        w_buf(q), (v, v_down, v_up, v_far), lambda i: w_send.at[q, i], lambda i: w_recv.at[q, i],
        here(u, v_up, z), here(u, v_down, z),
    )

    load_x.wait()
    gx[0]()
    for q in range(NQ):
        load_w[q].wait()
        if q not in SEND_W:
            gw(q)[0]()
    load_id.wait()
    for d in range(1, NY):
        start(remote(idg.at[u], idg.at[u], id_send.at[d - 1], id_recv.at[d - 1], here((u + d) % NY, v, z)))
    start(remote(block_of(u), xp, p_send.at[0], p_recv.at[0], partner))
    start(remote(idg.at[u], idp, p_send.at[1], p_recv.at[1], partner))

    gx[1]()
    gw(0)[1]()

    upper = (
        lax.broadcasted_iota(jnp.int32, (ROWS, ROWS), 0) <= lax.broadcasted_iota(jnp.int32, (ROWS, ROWS), 1)
    ).astype(BF)

    def route():
        for d in range(1, NY):
            src = (u + NY - d) % NY
            remote(idg.at[src], idg.at[src], id_send.at[d - 1], id_recv.at[d - 1], partner).wait_recv()
        for b in range(NY):
            owner = idg[b, 0:1, :]
            code = jnp.where((owner & 3) == u, (owner >> 2) * CAP + arrivals(owner, upper), -1)
            pick = (lax.broadcasted_iota(jnp.int32, (NX * CAP, ROWS), 0) == code).astype(BF)
            rows = dot(pick, xg[b * ROWS : (b + 1) * ROWS, :], 1, 0).astype(BF)
            for vv in range(NX):
                aout[vv, b * CAP : (b + 1) * CAP, :] = rows[vv * CAP : (vv + 1) * CAP]
            place_in = (
                lax.broadcasted_iota(jnp.int32, (NX * GROUP, ROWS), 0)
                == jnp.where(code < 0, -1, (code >> 5) * GROUP + b * CAP + (code & 31))
            ).astype(BF)
            slot_block = jnp.broadcast_to(idg[b, 1:2, :].astype(F32).astype(BF), (8, ROWS))
            chosen = dot(slot_block, place_in, 1, 1)
            for vv in range(NX):
                part = chosen[:, vv * GROUP : (vv + 1) * GROUP]
                sout[vv] = part if b == 0 else sout[vv] + part
        for d in range(1, NX):
            to = (v + d) % NX
            route_copy(d, to).start()
            slot_copy(d, to).start()
        ain[v] = aout[v]
        sin[v] = sout[v]

    def route_copy(d, to):
        return remote(aout.at[to], ain.at[v], f_send.at[d - 1], f_recv.at[d - 1], here(u, to, z))

    def slot_copy(d, to):
        return remote(sout.at[to], sin.at[v], g_send.at[d - 1], g_recv.at[d - 1], here(u, to, z))

    def row_block(f):
        r = f % NY
        return (u + ((r + 3) // 4) * ((r + 1) % 3 + 1)) % NY

    def ring_copy(f, direction, p):
        to = here(u, v, (z + 1) % NZ if direction == 0 else (z + NZ - 1) % NZ)
        return remote(
            rs.at[direction, f, p], rs.at[direction, f, p + odd],
            rs_send.at[direction, f, p], rs_recv.at[direction, f, p + odd], to,
        )

    def arrived(f, direction, p):
        remote(
            rs.at[direction, f, p], rs.at[direction, f, p],
            rs_send.at[direction, f, p], rs_recv.at[direction, f, p], partner,
        ).wait_recv()
        return rs[direction, f, p].astype(F32)

    def last_copy(f):
        return remote(
            rs.at[0, f, 2], bt.at[u % 2, f // NY], b_send.at[f], b_recv.at[u % 2, f // NY], there(row_block(f), v, z)
        )

    def product(f, root):
        rows = pl.ds(pl.multiple_of(row_block(f) * ROWS, ROWS), ROWS)
        return dot(xg[rows, :], wg[root // 2, f // NY], 1, 0)

    def in_turn(f):
        return (f >= 0) & (f < FLOWS)

    def first_direction(f):
        return f % 2

    def tile_step(i):
        @pl.when((odd == 0) & in_turn(i))
        def _():
            part = product(i, (z + 4) % NZ).astype(BF)
            for direction in range(2):
                @pl.when(first_direction(i) == direction)
                def _():
                    rs[direction, i, 0] = part
                    ring_copy(i, direction, 0).start()

        f3 = i - LAGS[1]

        @pl.when((odd == 1) & in_turn(f3))
        def _():
            for direction in range(2):
                root = (z + 3) % NZ if direction == 0 else (z + NZ - 3) % NZ
                part = product(f3, root)

                @pl.when(first_direction(f3) == direction)
                def _():
                    rs[direction, f3, 0] = (part + arrived(f3, direction, 0)).astype(BF)

                @pl.when(first_direction(f3) != direction)
                def _():
                    rs[direction, f3, 0] = part.astype(BF)

                ring_copy(f3, direction, 0).start()

        away = 2 - odd
        f1 = i - LAGS[2] - odd * (LAGS[3] - LAGS[2])

        @pl.when(in_turn(f1))
        def _():
            for direction in range(2):
                root = (z + away) % NZ if direction == 0 else (z + NZ - away) % NZ
                part = product(f1, root)
                rs[direction, f1, 1] = (part + arrived(f1, direction, 1)).astype(BF)
                ring_copy(f1, direction, 1).start()

        f0 = i - LAGS[4]

        @pl.when((odd == 0) & in_turn(f0))
        def _():
            part = product(f0, z)
            part = part + arrived(f0, 0, 2)
            rs[0, f0, 2] = (part + arrived(f0, 1, 2)).astype(BF)
            last_copy(f0).start()

    def shrink_part(c):
        if c == 0:
            load_shrink.wait()
            for d in range(1, NX):
                src = (v + NX - d) % NX
                remote(ain.at[src], ain.at[src], f_send.at[d - 1], f_recv.at[d - 1], partner).wait_recv()
                remote(sin.at[src], sin.at[src], g_send.at[d - 1], g_recv.at[d - 1], partner).wait_recv()
            total[...] = jnp.zeros_like(total)

        count = SLOTS // PARTS
        projected = dot(
            shrink[pl.ds(c * (count * RANK), count * RANK), :], ain[...].reshape(NX * GROUP, WIDTH), 1, 1
        )
        for vv in range(NX):
            slots = sin[vv, 0:1, :].astype(jnp.int32) - c * count
            sums = total[vv]
            for k in range(count):
                sums = sums + jnp.where(
                    slots == k, projected[k * RANK : (k + 1) * RANK, vv * GROUP : (vv + 1) * GROUP], 0.0
                )
            total[vv] = sums

        if c == PARTS - 1:
            pin[z] = total[...].astype(BF)
            for d in range(1, NZ):
                sum_copy(d).start()

    def sum_copy(d):
        return remote(pin.at[z], pin.at[z], z_send.at[d - 1], z_recv.at[d - 1], here(u, v, (z + d) % NZ))

    def return_copy(vv, b):
        return remote(
            low.at[vv, pl.ds(b * CAP, CAP), :], lin.at[dp], r_send.at[vv, b], r_recv.at[dp], there(b, vv, z)
        )

    def expand_part(vv):
        if vv == 0:
            load_expand.wait()
            for d in range(1, NZ):
                src = (z + NZ - d) % NZ
                remote(pin.at[src], pin.at[src], z_send.at[d - 1], z_recv.at[d - 1], partner).wait_recv()

        sums = pin[0, vv].astype(F32)
        for k in range(1, NZ):
            sums = sums + pin[k, vv].astype(F32)
        slots = sin[vv, 0:1, :].astype(jnp.int32)
        for k in range(SLOTS):
            spread[k * RANK : (k + 1) * RANK, :] = jnp.where(slots == k, sums, 0.0).astype(BF)
        low[vv] = dot(spread[...], expand[...], 0, 0).astype(BF)
        for b in range(NY):
            return_copy(vv, b).start()

    def round_of(j, carry):
        @pl.when(in_turn(j) & (j % NY == 0))
        def _():
            gw(j // NY)[5]()

        for f in range(1, NY):
            pl.when(j == f)(gx[1 + f])

        for chunk, at in PASS_W.items():
            pl.when(j == at)(gw(chunk)[1])
        for chunk, at in SEND_W.items():
            pl.when(j == at)(gw(chunk)[0])

        tile_step(j)

        pl.when(j == ROUTE_AT)(route)
        for c in range(PARTS):
            pl.when(j == SHRINK_AT[c])(functools.partial(shrink_part, c))
        for vv in range(NX):
            pl.when(j == EXPAND_AT[vv])(functools.partial(expand_part, vv))
        return carry

    lax.fori_loop(0, ROUNDS, round_of, 0)

    remote(block_of(u), xp, p_send.at[0], p_recv.at[0], partner).wait_recv()
    remote(idg.at[u], idp, p_send.at[1], p_recv.at[1], partner).wait_recv()
    owner = idp[0:1, :]
    code = owner * CAP + arrivals(owner, upper)
    pick = (lax.broadcasted_iota(jnp.int32, (OWNERS * CAP, ROWS), 0) == code).astype(BF)
    for o in range(OWNERS):
        remote(lin.at[o], lin.at[o], r_send.at[0, 0], r_recv.at[o], partner).wait_recv()
    got = lin[...].reshape(OWNERS * CAP, WIDTH)
    for q in range(NQ):
        for p in range(2):
            remote(bt.at[p, q], bt.at[p, q], b_send.at[q], b_recv.at[p, q], partner).wait_recv()
    for c in range(WIDTH // 256):
        cols = slice(c * 256, (c + 1) * 256)
        rows = dot(pick, got[:, cols], 0, 0)
        p, q = (c * 256) // COLS, ((c * 256) % COLS) // CW
        base = jnp.concatenate([bt[p, q + k] for k in range(256 // CW)], axis=1)
        out_ref[:, cols] = (xp[:, cols].astype(F32) + base.astype(F32) + rows).astype(BF)

    for copy in started:
        copy.wait_send()
    gx[6]()
    for q in range(NQ):
        gw(q)[6]()

    def drain_flow(f, carry):
        for direction in range(2):
            pl.when((odd == 1) | (first_direction(f) == direction))(
                lambda: ring_copy(f, direction, 0).wait_send()
            )
            ring_copy(f, direction, 1).wait_send()
        pl.when(odd == 0)(lambda: last_copy(f).wait_send())
        return carry

    lax.fori_loop(0, FLOWS, drain_flow, 0)
    for d in range(1, NX):
        route_copy(d, (v + d) % NX).wait_send()
        slot_copy(d, (v + d) % NX).wait_send()
    for d in range(1, NZ):
        sum_copy(d).wait_send()
    for vv in range(NX):
        for b in range(NY):
            return_copy(vv, b).wait_send()


def local_part(hidden_states, base_weight, shrink_weight, expand_weight, owner_ids, adapter_slots):
    ids = jnp.concatenate(
        [owner_ids.reshape(1, ROWS), adapter_slots.reshape(1, ROWS), jnp.zeros((6, ROWS), jnp.int32)], axis=0
    )
    dma = pltpu.SemaphoreType.DMA
    any_spec = pl.BlockSpec(memory_space=pl.ANY)
    out = pl.pallas_call(
        kernel,
        out_shape=jax.ShapeDtypeStruct((ROWS, WIDTH), BF),
        in_specs=[any_spec] * 5,
        out_specs=pl.BlockSpec(memory_space=pltpu.VMEM),
        scratch_shapes=[
            pltpu.VMEM((NY * ROWS, WIDTH), BF),
            pltpu.VMEM((NX, NQ, WIDTH, CW), BF),
            pltpu.VMEM((NY, 8, ROWS), jnp.int32),
            pltpu.VMEM((2, FLOWS, STEPS, ROWS, CW), BF),
            pltpu.VMEM((2, NQ, ROWS, CW), BF),
            pltpu.VMEM((ROWS, WIDTH), BF),
            pltpu.VMEM((8, ROWS), jnp.int32),
            pltpu.VMEM((NX, GROUP, WIDTH), BF),
            pltpu.VMEM((NX, 8, GROUP), F32),
            pltpu.VMEM((NX, GROUP, WIDTH), BF),
            pltpu.VMEM((NX, 8, GROUP), F32),
            pltpu.VMEM((SLOTS * RANK, WIDTH), BF),
            pltpu.VMEM((SLOTS * RANK, WIDTH), BF),
            pltpu.VMEM((NX, RANK, GROUP), F32),
            pltpu.VMEM((NZ, NX, RANK, GROUP), BF),
            pltpu.VMEM((SLOTS * RANK, GROUP), BF),
            pltpu.VMEM((NX, GROUP, WIDTH), BF),
            pltpu.VMEM((OWNERS, CAP, WIDTH), BF),
            dma((4 + NQ,)),
            dma((6,)), dma((6,)),
            dma((NY - 1,)), dma((NY - 1,)),
            dma((NQ, 6)), dma((NQ, 6)),
            dma((2,)), dma((2,)),
            dma((NX - 1,)), dma((NX - 1,)),
            dma((NX - 1,)), dma((NX - 1,)),
            dma((NZ - 1,)), dma((NZ - 1,)),
            dma((NX, NY)), dma((OWNERS,)),
            dma((FLOWS,)), dma((2, NQ)),
            dma((2, FLOWS, STEPS)), dma((2, FLOWS, STEPS)),
        ],
        compiler_params=pltpu.CompilerParams(
            collective_id=0, has_side_effects=True, vmem_limit_bytes=56 << 20
        ),
    )(
        hidden_states[0],
        base_weight[0],
        shrink_weight[0].reshape(SLOTS * RANK, WIDTH),
        expand_weight[0].reshape(SLOTS * RANK, WIDTH),
        ids,
    )
    return out[None]


def solution(mesh):
    return jax.shard_map(
        local_part,
        mesh=mesh,
        in_specs=(
            P("section", "dp", "tensor"),
            P("section", "tensor", "dp"),
            P("section", "dp", None, "tensor"),
            P("section", "dp", None, "tensor"),
            P("section", "dp", None),
            P("section", "dp"),
        ),
        out_specs=P("section", "dp", "tensor"),
        check_vma=False,
    )
```

```python
import functools

import jax
import jax.numpy as jnp
from jax import lax
from jax.experimental import pallas as pl
from jax.experimental.pallas import tpu as pltpu
from jax.sharding import PartitionSpec as P

MESH = pl.DeviceIdType.MESH
NX, NY, NZ = 4, 4, 8
ROWS, WIDTH, COLS = 256, 1024, 512
OWNERS, CAP, SLOTS, RANK = 16, 32, 64, 16
NQ = 4
CW = COLS // NQ
GROUP = NY * CAP
FLOWS = NQ * NY
STEPS = 3
GAP = 1
PERIOD = NY + GAP
LAGS = (0, 2, 4, 6, 8)
ROUNDS = NQ * PERIOD - GAP + LAGS[4]
SEND_W = {2: 1, 3: 6}
PASS_W = {1: 1, 2: 6, 3: 11}
ROUTE_AT = 11
SHRINK_AT = (17, 17, 18, 18)
EXPAND_AT = (20, 21, 22, 23)
PARTS = 4
BF, F32 = jnp.bfloat16, jnp.float32


def remote(src, dst, send, recv, device):
    return pltpu.make_async_remote_copy(
        src_ref=src, dst_ref=dst, send_sem=send, recv_sem=recv, device_id=device, device_id_type=MESH
    )


def dot(a, b, ca, cb):
    return lax.dot_general(a, b, (((ca,), (cb,)), ((), ())), preferred_element_type=F32)


def arrivals(owner, upper):
    hits = lax.broadcasted_iota(jnp.int32, (OWNERS, ROWS), 0) == owner
    count = dot(hits.astype(BF), upper, 1, 0)
    return (jnp.sum(jnp.where(hits, count, 0.0), axis=0, keepdims=True) - 1.0).astype(jnp.int32)


def kernel(
    x_hbm, w_hbm, shrink_hbm, expand_hbm, ids_hbm, out_ref,
    xg, wg, idg, rs, bt, xp, idp, aout, sout, ain, sin, shrink, expand, total, pin, spread, low, lin, acc,
    loc_sem, x_send, x_recv, id_send, id_recv, w_send, w_recv, p_send, p_recv, f_send, f_recv,
    g_send, g_recv, z_send, z_recv, r_send, r_recv, b_send, b_recv, rs_send, rs_recv,
):
    s = lax.axis_index("section")
    dp = lax.axis_index("dp")
    z = lax.axis_index("tensor")
    x, y = dp // NY, dp % NY
    u, v = y, x
    place = lambda uu, vv: vv * NY + uu
    here = lambda uu, vv, zz: (s, place(uu, vv), zz)
    there = lambda uu, vv, zz: (1 - s, place(uu, vv), zz)
    odd = (z + u // 2) % 2
    partner = (1 - s, dp, z)

    def local(src, dst, i):
        return pltpu.make_async_copy(src, dst, loc_sem.at[i])

    block_of = lambda b: xg.at[pl.ds(pl.multiple_of(b * ROWS, ROWS), ROWS), :]
    load_x = local(x_hbm, block_of(u), 0)
    load_id = local(ids_hbm, idg.at[u], 1)
    load_w = [local(w_hbm.at[:, pl.ds(q * CW, CW)], wg.at[v, q], 4 + q) for q in range(NQ)]
    load_shrink = local(shrink_hbm, shrink, 2)
    load_expand = local(expand_hbm, expand, 3)
    load_x.start()
    for q in range(NQ):
        load_w[q].start()
    load_id.start()

    barrier = pltpu.get_barrier_semaphore()
    peers = [here((u + d) % NY, v, z) for d in range(1, NY)]
    peers += [here(u, (v + d) % NX, z) for d in range(1, NX)]
    peers += [here(u, v, (z + d) % NZ) for d in range(1, NZ)]
    peers += [(1 - s, o, z) for o in range(OWNERS)]
    for peer in peers:
        pl.semaphore_signal(barrier, inc=1, device_id=peer, device_id_type=MESH)
    pl.semaphore_wait(barrier, len(peers))

    started = []

    def start(copy):
        copy.start()
        started.append(copy)

    def gather(buf, slots, send, recv, up, down):
        mine, below, above, far = slots
        sends = [remote(buf(mine, h), buf(mine, h), send(i), recv(i), to) for i, (h, to) in enumerate(
            [(0, up), (1, down), (1, up), (0, down)])]
        arrive = [remote(buf(slot, h), buf(slot, h), send(i), recv(i), up) for i, (slot, h) in enumerate(
            [(below, 0), (above, 1), (below, 1), (above, 0)])]
        pass_up = remote(buf(below, 0), buf(below, 0), send(4), recv(4), up)
        pass_down = remote(buf(above, 1), buf(above, 1), send(5), recv(5), down)
        far_up = remote(buf(far, 0), buf(far, 0), send(4), recv(4), up)
        far_down = remote(buf(far, 1), buf(far, 1), send(5), recv(5), down)

        def first():
            for copy in sends:
                copy.start()

        def forward():
            arrive[0].wait_recv()
            pass_up.start()
            arrive[1].wait_recv()
            pass_down.start()

        def finish_below():
            arrive[2].wait_recv()

        def finish_above():
            arrive[3].wait_recv()

        def finish_far():
            far_up.wait_recv()
            far_down.wait_recv()

        def finish():
            finish_below()
            finish_above()
            finish_far()

        def drain():
            for copy in sends:
                copy.wait_send()
            pass_up.wait_send()
            pass_down.wait_send()

        return first, forward, finish_below, finish_above, finish_far, finish, drain

    u_up, u_down, u_far = (u + 1) % NY, (u + NY - 1) % NY, (u + 2) % NY
    v_up, v_down, v_far = (v + 1) % NX, (v + NX - 1) % NX, (v + 2) % NX
    x_buf = lambda slot, h: xg.at[pl.ds(pl.multiple_of(slot * ROWS + h * (ROWS // 2), ROWS // 2), ROWS // 2), :]
    w_buf = lambda q: lambda slot, h: wg.at[slot, q, pl.ds(h * (WIDTH // 2), WIDTH // 2), :]
    gx = gather(
        x_buf, (u, u_down, u_up, u_far), lambda i: x_send.at[i], lambda i: x_recv.at[i],
        here(u_up, v, z), here(u_down, v, z),
    )
    gw = lambda q: gather(
        w_buf(q), (v, v_down, v_up, v_far), lambda i: w_send.at[q, i], lambda i: w_recv.at[q, i],
        here(u, v_up, z), here(u, v_down, z),
    )

    load_x.wait()
    gx[0]()
    load_w[0].wait()
    gw(0)[0]()
    load_id.wait()
    for d in range(1, NY):
        start(remote(idg.at[u], idg.at[u], id_send.at[d - 1], id_recv.at[d - 1], here((u + d) % NY, v, z)))
    start(remote(block_of(u), xp, p_send.at[0], p_recv.at[0], partner))
    start(remote(idg.at[u], idp, p_send.at[1], p_recv.at[1], partner))

    load_shrink.start()
    load_expand.start()
    for q in range(1, NQ):
        load_w[q].wait()
    gw(0)[1]()
    gw(1)[0]()
    gx[1]()

    upper = (
        lax.broadcasted_iota(jnp.int32, (ROWS, ROWS), 0) <= lax.broadcasted_iota(jnp.int32, (ROWS, ROWS), 1)
    ).astype(BF)

    def route():
        for d in range(1, NY):
            src = (u + NY - d) % NY
            remote(idg.at[src], idg.at[src], id_send.at[d - 1], id_recv.at[d - 1], partner).wait_recv()
        for b in range(NY):
            owner = idg[b, 0:1, :]
            code = jnp.where((owner & 3) == u, (owner >> 2) * CAP + arrivals(owner, upper), -1)
            pick = (lax.broadcasted_iota(jnp.int32, (NX * CAP, ROWS), 0) == code).astype(BF)
            rows = dot(pick, xg[b * ROWS : (b + 1) * ROWS, :], 1, 0).astype(BF)
            for vv in range(NX):
                aout[vv, b * CAP : (b + 1) * CAP, :] = rows[vv * CAP : (vv + 1) * CAP]
            place_in = (
                lax.broadcasted_iota(jnp.int32, (NX * GROUP, ROWS), 0)
                == jnp.where(code < 0, -1, (code >> 5) * GROUP + b * CAP + (code & 31))
            ).astype(BF)
            slot_block = jnp.broadcast_to(idg[b, 1:2, :].astype(F32).astype(BF), (8, ROWS))
            chosen = dot(slot_block, place_in, 1, 1)
            for vv in range(NX):
                part = chosen[:, vv * GROUP : (vv + 1) * GROUP]
                sout[vv] = part if b == 0 else sout[vv] + part
        for d in range(1, NX):
            to = (v + d) % NX
            route_copy(d, to).start()
            slot_copy(d, to).start()
        ain[v] = aout[v]
        sin[v] = sout[v]

    def route_copy(d, to):
        return remote(aout.at[to], ain.at[v], f_send.at[d - 1], f_recv.at[d - 1], here(u, to, z))

    def slot_copy(d, to):
        return remote(sout.at[to], sin.at[v], g_send.at[d - 1], g_recv.at[d - 1], here(u, to, z))

    def row_block(f):
        r = f % NY
        return (u + ((r + 3) // 4) * ((r + 1) % 3 + 1)) % NY

    def ring_copy(f, direction, p):
        to = here(u, v, (z + 1) % NZ if direction == 0 else (z + NZ - 1) % NZ)
        return remote(
            rs.at[direction, f, p], rs.at[direction, f, p + odd],
            rs_send.at[direction, f, p], rs_recv.at[direction, f, p + odd], to,
        )

    def arrived(f, direction, p):
        remote(
            rs.at[direction, f, p], rs.at[direction, f, p],
            rs_send.at[direction, f, p], rs_recv.at[direction, f, p], partner,
        ).wait_recv()
        return rs[direction, f, p].astype(F32)

    def last_copy(f):
        return remote(
            rs.at[0, f, 2], bt.at[u % 2, f // NY], b_send.at[f], b_recv.at[u % 2, f // NY], there(row_block(f), v, z)
        )

    def product(f, root):
        rows = pl.ds(pl.multiple_of(row_block(f) * ROWS, ROWS), ROWS)
        return dot(xg[rows, :], wg[root // 2, f // NY], 1, 0)

    def in_turn(i):
        return (i >= 0) & (i < NQ * PERIOD) & (i % PERIOD < NY)

    def flow(i):
        return (i // PERIOD) * NY + i % PERIOD

    def first_direction(f):
        return f % 2

    def tile_step(i):
        @pl.when((odd == 0) & in_turn(i))
        def _():
            f4 = flow(i)
            part = product(f4, (z + 4) % NZ).astype(BF)
            for direction in range(2):
                @pl.when(first_direction(f4) == direction)
                def _():
                    rs[direction, f4, 0] = part
                    ring_copy(f4, direction, 0).start()

        i3 = i - LAGS[1]
        f3 = flow(i3)

        @pl.when((odd == 1) & in_turn(i3))
        def _():
            for direction in range(2):
                root = (z + 3) % NZ if direction == 0 else (z + NZ - 3) % NZ
                part = product(f3, root)

                @pl.when(first_direction(f3) == direction)
                def _():
                    rs[direction, f3, 0] = (part + arrived(f3, direction, 0)).astype(BF)

                @pl.when(first_direction(f3) != direction)
                def _():
                    rs[direction, f3, 0] = part.astype(BF)

                ring_copy(f3, direction, 0).start()

        away = 2 - odd
        i1 = i - LAGS[2] - odd * (LAGS[3] - LAGS[2])
        f1 = flow(i1)

        @pl.when(in_turn(i1))
        def _():
            for direction in range(2):
                root = (z + away) % NZ if direction == 0 else (z + NZ - away) % NZ
                part = product(f1, root)
                rs[direction, f1, 1] = (part + arrived(f1, direction, 1)).astype(BF)
                ring_copy(f1, direction, 1).start()

        i0 = i - LAGS[4]
        f0 = flow(i0)

        @pl.when((odd == 0) & in_turn(i0))
        def _():
            part = product(f0, z)
            part = part + arrived(f0, 0, 2)
            rs[0, f0, 2] = (part + arrived(f0, 1, 2)).astype(BF)
            last_copy(f0).start()

    def shrink_part(c):
        if c == 0:
            load_shrink.wait()
            for d in range(1, NX):
                src = (v + NX - d) % NX
                remote(ain.at[src], ain.at[src], f_send.at[d - 1], f_recv.at[d - 1], partner).wait_recv()
                remote(sin.at[src], sin.at[src], g_send.at[d - 1], g_recv.at[d - 1], partner).wait_recv()
            total[...] = jnp.zeros_like(total)

        count = SLOTS // PARTS
        projected = dot(
            shrink[pl.ds(c * (count * RANK), count * RANK), :], ain[...].reshape(NX * GROUP, WIDTH), 1, 1
        )
        for vv in range(NX):
            slots = sin[vv, 0:1, :].astype(jnp.int32) - c * count
            sums = total[vv]
            for k in range(count):
                sums = sums + jnp.where(
                    slots == k, projected[k * RANK : (k + 1) * RANK, vv * GROUP : (vv + 1) * GROUP], 0.0
                )
            total[vv] = sums

        if c == PARTS - 1:
            pin[z] = total[...].astype(BF)
            for d in range(1, NZ):
                sum_copy(d).start()

    def sum_copy(d):
        return remote(pin.at[z], pin.at[z], z_send.at[d - 1], z_recv.at[d - 1], here(u, v, (z + d) % NZ))

    def return_copy(vv, b):
        return remote(
            low.at[vv, pl.ds(b * CAP, CAP), :], lin.at[dp], r_send.at[vv, b], r_recv.at[dp], there(b, vv, z)
        )

    def expand_part(vv):
        if vv == 0:
            load_expand.wait()
            for d in range(1, NZ):
                src = (z + NZ - d) % NZ
                remote(pin.at[src], pin.at[src], z_send.at[d - 1], z_recv.at[d - 1], partner).wait_recv()

        sums = pin[0, vv].astype(F32)
        for k in range(1, NZ):
            sums = sums + pin[k, vv].astype(F32)
        slots = sin[vv, 0:1, :].astype(jnp.int32)
        for k in range(SLOTS):
            spread[k * RANK : (k + 1) * RANK, :] = jnp.where(slots == k, sums, 0.0).astype(BF)
        low[vv] = dot(spread[...], expand[...], 0, 0).astype(BF)
        for b in range(NY):
            return_copy(vv, b).start()

    def round_of(j, carry):
        @pl.when(in_turn(j) & (j % PERIOD == 0))
        def _():
            gw(j // PERIOD)[5]()

        for f in range(1, NY):
            pl.when(j == f)(gx[1 + f])

        for chunk, at in PASS_W.items():
            pl.when(j == at)(gw(chunk)[1])
        for chunk, at in SEND_W.items():
            pl.when(j == at)(gw(chunk)[0])

        tile_step(j)

        pl.when(j == ROUTE_AT)(route)
        for c in range(PARTS):
            pl.when(j == SHRINK_AT[c])(functools.partial(shrink_part, c))
        for vv in range(NX):
            pl.when(j == EXPAND_AT[vv])(functools.partial(expand_part, vv))
        return carry

    lax.fori_loop(0, ROUNDS, round_of, 0)

    remote(block_of(u), xp, p_send.at[0], p_recv.at[0], partner).wait_recv()
    remote(idg.at[u], idp, p_send.at[1], p_recv.at[1], partner).wait_recv()
    owner = idp[0:1, :]
    code = owner * CAP + arrivals(owner, upper)
    pick = (lax.broadcasted_iota(jnp.int32, (OWNERS * CAP, ROWS), 0) == code).astype(BF)
    for copy in started:
        copy.wait_send()
    gx[6]()
    for q in range(NQ):
        gw(q)[6]()
    for d in range(1, NX):
        route_copy(d, (v + d) % NX).wait_send()
        slot_copy(d, (v + d) % NX).wait_send()
    for d in range(1, NZ):
        sum_copy(d).wait_send()

    def drain_flow(f, carry):
        for direction in range(2):
            pl.when((odd == 1) | (first_direction(f) == direction))(
                lambda: ring_copy(f, direction, 0).wait_send()
            )
            ring_copy(f, direction, 1).wait_send()
        pl.when(odd == 0)(lambda: last_copy(f).wait_send())
        return carry

    lax.fori_loop(0, FLOWS - NY, drain_flow, 0)

    for o in range(OWNERS):
        remote(lin.at[o], lin.at[o], r_send.at[0, 0], r_recv.at[o], partner).wait_recv()
    for c in range(WIDTH // 256):
        cols = slice(c * 256, (c + 1) * 256)
        rows = dot(pick, lin[:, :, cols].reshape(OWNERS * CAP, 256), 0, 0)
        acc[:, cols] = xp[:, cols].astype(F32) + rows
    for vv in range(NX):
        for b in range(NY):
            return_copy(vv, b).wait_send()
    for q in range(NQ):
        for p in range(2):
            remote(bt.at[p, q], bt.at[p, q], b_send.at[q], b_recv.at[p, q], partner).wait_recv()
            cols = slice(p * COLS + q * CW, p * COLS + (q + 1) * CW)
            out_ref[:, cols] = (acc[:, cols] + bt[p, q].astype(F32)).astype(BF)
    lax.fori_loop(FLOWS - NY, FLOWS, drain_flow, 0)


def local_part(hidden_states, base_weight, shrink_weight, expand_weight, owner_ids, adapter_slots):
    ids = jnp.concatenate(
        [owner_ids.reshape(1, ROWS), adapter_slots.reshape(1, ROWS), jnp.zeros((6, ROWS), jnp.int32)], axis=0
    )
    dma = pltpu.SemaphoreType.DMA
    any_spec = pl.BlockSpec(memory_space=pl.ANY)
    out = pl.pallas_call(
        kernel,
        out_shape=jax.ShapeDtypeStruct((ROWS, WIDTH), BF),
        in_specs=[any_spec] * 5,
        out_specs=pl.BlockSpec(memory_space=pltpu.VMEM),
        scratch_shapes=[
            pltpu.VMEM((NY * ROWS, WIDTH), BF),
            pltpu.VMEM((NX, NQ, WIDTH, CW), BF),
            pltpu.VMEM((NY, 8, ROWS), jnp.int32),
            pltpu.VMEM((2, FLOWS, STEPS, ROWS, CW), BF),
            pltpu.VMEM((2, NQ, ROWS, CW), BF),
            pltpu.VMEM((ROWS, WIDTH), BF),
            pltpu.VMEM((8, ROWS), jnp.int32),
            pltpu.VMEM((NX, GROUP, WIDTH), BF),
            pltpu.VMEM((NX, 8, GROUP), F32),
            pltpu.VMEM((NX, GROUP, WIDTH), BF),
            pltpu.VMEM((NX, 8, GROUP), F32),
            pltpu.VMEM((SLOTS * RANK, WIDTH), BF),
            pltpu.VMEM((SLOTS * RANK, WIDTH), BF),
            pltpu.VMEM((NX, RANK, GROUP), F32),
            pltpu.VMEM((NZ, NX, RANK, GROUP), BF),
            pltpu.VMEM((SLOTS * RANK, GROUP), BF),
            pltpu.VMEM((NX, GROUP, WIDTH), BF),
            pltpu.VMEM((OWNERS, CAP, WIDTH), BF),
            pltpu.VMEM((ROWS, WIDTH), F32),
            dma((4 + NQ,)),
            dma((6,)), dma((6,)),
            dma((NY - 1,)), dma((NY - 1,)),
            dma((NQ, 6)), dma((NQ, 6)),
            dma((2,)), dma((2,)),
            dma((NX - 1,)), dma((NX - 1,)),
            dma((NX - 1,)), dma((NX - 1,)),
            dma((NZ - 1,)), dma((NZ - 1,)),
            dma((NX, NY)), dma((OWNERS,)),
            dma((FLOWS,)), dma((2, NQ)),
            dma((2, FLOWS, STEPS)), dma((2, FLOWS, STEPS)),
        ],
        compiler_params=pltpu.CompilerParams(
            collective_id=0, has_side_effects=True, vmem_limit_bytes=56 << 20
        ),
    )(
        hidden_states[0],
        base_weight[0],
        shrink_weight[0].reshape(SLOTS * RANK, WIDTH),
        expand_weight[0].reshape(SLOTS * RANK, WIDTH),
        ids,
    )
    return out[None]


def solution(mesh):
    return jax.shard_map(
        local_part,
        mesh=mesh,
        in_specs=(
            P("section", "dp", "tensor"),
            P("section", "tensor", "dp"),
            P("section", "dp", None, "tensor"),
            P("section", "dp", None, "tensor"),
            P("section", "dp", None),
            P("section", "dp"),
        ),
        out_specs=P("section", "dp", "tensor"),
        check_vma=False,
    )
```

```python
import functools

import jax
import jax.numpy as jnp
from jax import lax
from jax.experimental import pallas as pl
from jax.experimental.pallas import tpu as pltpu
from jax.sharding import PartitionSpec as P

MESH = pl.DeviceIdType.MESH
NX, NY, NZ = 4, 4, 8
ROWS, WIDTH, COLS = 256, 1024, 512
OWNERS, CAP, SLOTS, RANK = 16, 32, 64, 16
NQ = 4
CW = COLS // NQ
GROUP = NY * CAP
FLOWS = NQ * NY
STEPS = 3
GAP = 1
PERIOD = NY + GAP
LAGS = (0, 2, 4, 6, 8)
ROUNDS = NQ * PERIOD - GAP + LAGS[4]
SEND_W = {2: 1, 3: 6}
PASS_W = {1: 1, 2: 6, 3: 11}
ROUTE_AT = 11
SHRINK_AT = (17, 17, 18, 18)
EXPAND_AT = (20, 21, 22, 23)
PARTS = 4
BF, F32 = jnp.bfloat16, jnp.float32


def remote(src, dst, send, recv, device):
    return pltpu.make_async_remote_copy(
        src_ref=src, dst_ref=dst, send_sem=send, recv_sem=recv, device_id=device, device_id_type=MESH
    )


def dot(a, b, ca, cb):
    return lax.dot_general(a, b, (((ca,), (cb,)), ((), ())), preferred_element_type=F32)


def arrivals(owner, upper):
    hits = lax.broadcasted_iota(jnp.int32, (OWNERS, ROWS), 0) == owner
    count = dot(hits.astype(BF), upper, 1, 0)
    return (jnp.sum(jnp.where(hits, count, 0.0), axis=0, keepdims=True) - 1.0).astype(jnp.int32)


def kernel(
    x_hbm, w_hbm, shrink_hbm, expand_hbm, ids_hbm, out_ref,
    xg, wg, idg, rs, bt, xp, idp, aout, sout, ain, sin, shrink, expand, total, pin, spread, low, lin, acc,
    loc_sem, x_send, x_recv, id_send, id_recv, w_send, w_recv, p_send, p_recv, f_send, f_recv,
    g_send, g_recv, z_send, z_recv, r_send, r_recv, b_send, b_recv, rs_send, rs_recv,
):
    s = lax.axis_index("section")
    dp = lax.axis_index("dp")
    z = lax.axis_index("tensor")
    x, y = dp // NY, dp % NY
    u, v = y, x
    place = lambda uu, vv: vv * NY + uu
    here = lambda uu, vv, zz: (s, place(uu, vv), zz)
    there = lambda uu, vv, zz: (1 - s, place(uu, vv), zz)
    odd = (z + u // 2) % 2
    partner = (1 - s, dp, z)

    def local(src, dst, i):
        return pltpu.make_async_copy(src, dst, loc_sem.at[i])

    block_of = lambda b: xg.at[pl.ds(pl.multiple_of(b * ROWS, ROWS), ROWS), :]
    load_x = local(x_hbm, block_of(u), 0)
    load_id = local(ids_hbm, idg.at[u], 1)
    load_w = [local(w_hbm.at[:, pl.ds(q * CW, CW)], wg.at[v, q], 4 + q) for q in range(NQ)]
    load_shrink = local(shrink_hbm, shrink, 2)
    load_expand = local(expand_hbm, expand, 3)
    load_x.start()
    for q in range(NQ):
        load_w[q].start()
    load_id.start()

    barrier = pltpu.get_barrier_semaphore()
    peers = [here((u + d) % NY, v, z) for d in range(1, NY)]
    peers += [here(u, (v + d) % NX, z) for d in range(1, NX)]
    peers += [here(u, v, (z + d) % NZ) for d in range(1, NZ)]
    peers += [(1 - s, o, z) for o in range(OWNERS)]
    for peer in peers:
        pl.semaphore_signal(barrier, inc=1, device_id=peer, device_id_type=MESH)
    pl.semaphore_wait(barrier, len(peers))

    started = []

    def start(copy):
        copy.start()
        started.append(copy)

    def gather(buf, slots, send, recv, up, down):
        mine, below, above, far = slots
        sends = [remote(buf(mine, h), buf(mine, h), send(i), recv(i), to) for i, (h, to) in enumerate(
            [(0, up), (1, down), (1, up), (0, down)])]
        arrive = [remote(buf(slot, h), buf(slot, h), send(i), recv(i), up) for i, (slot, h) in enumerate(
            [(below, 0), (above, 1), (below, 1), (above, 0)])]
        pass_up = remote(buf(below, 0), buf(below, 0), send(4), recv(4), up)
        pass_down = remote(buf(above, 1), buf(above, 1), send(5), recv(5), down)
        far_up = remote(buf(far, 0), buf(far, 0), send(4), recv(4), up)
        far_down = remote(buf(far, 1), buf(far, 1), send(5), recv(5), down)

        def first():
            for copy in sends:
                copy.start()

        def forward():
            arrive[0].wait_recv()
            pass_up.start()
            arrive[1].wait_recv()
            pass_down.start()

        def finish_below():
            arrive[2].wait_recv()

        def finish_above():
            arrive[3].wait_recv()

        def finish_far():
            far_up.wait_recv()
            far_down.wait_recv()

        def finish():
            finish_below()
            finish_above()
            finish_far()

        def drain():
            for copy in sends:
                copy.wait_send()
            pass_up.wait_send()
            pass_down.wait_send()

        return first, forward, finish_below, finish_above, finish_far, finish, drain

    u_up, u_down, u_far = (u + 1) % NY, (u + NY - 1) % NY, (u + 2) % NY
    v_up, v_down, v_far = (v + 1) % NX, (v + NX - 1) % NX, (v + 2) % NX
    x_buf = lambda slot, h: xg.at[pl.ds(pl.multiple_of(slot * ROWS + h * (ROWS // 2), ROWS // 2), ROWS // 2), :]
    w_buf = lambda q: lambda slot, h: wg.at[slot, q, pl.ds(h * (WIDTH // 2), WIDTH // 2), :]
    gx = gather(
        x_buf, (u, u_down, u_up, u_far), lambda i: x_send.at[i], lambda i: x_recv.at[i],
        here(u_up, v, z), here(u_down, v, z),
    )
    gw = lambda q: gather(
        w_buf(q), (v, v_down, v_up, v_far), lambda i: w_send.at[q, i], lambda i: w_recv.at[q, i],
        here(u, v_up, z), here(u, v_down, z),
    )

    load_x.wait()
    gx[0]()
    load_w[0].wait()
    gw(0)[0]()
    load_id.wait()
    for d in range(1, NY):
        start(remote(idg.at[u], idg.at[u], id_send.at[d - 1], id_recv.at[d - 1], here((u + d) % NY, v, z)))

    load_shrink.start()
    load_expand.start()
    for q in range(1, NQ):
        load_w[q].wait()
    gw(0)[1]()
    gw(1)[0]()
    gx[1]()
    start(remote(block_of(u), xp, p_send.at[0], p_recv.at[0], partner))
    start(remote(idg.at[u], idp, p_send.at[1], p_recv.at[1], partner))

    upper = (
        lax.broadcasted_iota(jnp.int32, (ROWS, ROWS), 0) <= lax.broadcasted_iota(jnp.int32, (ROWS, ROWS), 1)
    ).astype(BF)

    def route():
        for d in range(1, NY):
            src = (u + NY - d) % NY
            remote(idg.at[src], idg.at[src], id_send.at[d - 1], id_recv.at[d - 1], partner).wait_recv()
        for b in range(NY):
            owner = idg[b, 0:1, :]
            code = jnp.where((owner & 3) == u, (owner >> 2) * CAP + arrivals(owner, upper), -1)
            pick = (lax.broadcasted_iota(jnp.int32, (NX * CAP, ROWS), 0) == code).astype(BF)
            rows = dot(pick, xg[b * ROWS : (b + 1) * ROWS, :], 1, 0).astype(BF)
            for vv in range(NX):
                aout[vv, b * CAP : (b + 1) * CAP, :] = rows[vv * CAP : (vv + 1) * CAP]
            place_in = (
                lax.broadcasted_iota(jnp.int32, (NX * GROUP, ROWS), 0)
                == jnp.where(code < 0, -1, (code >> 5) * GROUP + b * CAP + (code & 31))
            ).astype(BF)
            slot_block = jnp.broadcast_to(idg[b, 1:2, :].astype(F32).astype(BF), (8, ROWS))
            chosen = dot(slot_block, place_in, 1, 1)
            for vv in range(NX):
                part = chosen[:, vv * GROUP : (vv + 1) * GROUP]
                sout[vv] = part if b == 0 else sout[vv] + part
        for d in range(1, NX):
            to = (v + d) % NX
            route_copy(d, to).start()
            slot_copy(d, to).start()
        ain[v] = aout[v]
        sin[v] = sout[v]

    def route_copy(d, to):
        return remote(aout.at[to], ain.at[v], f_send.at[d - 1], f_recv.at[d - 1], here(u, to, z))

    def slot_copy(d, to):
        return remote(sout.at[to], sin.at[v], g_send.at[d - 1], g_recv.at[d - 1], here(u, to, z))

    def row_block(f):
        r = f % NY
        return (u + ((r + 3) // 4) * ((r + 1) % 3 + 1)) % NY

    def ring_copy(f, direction, p):
        to = here(u, v, (z + 1) % NZ if direction == 0 else (z + NZ - 1) % NZ)
        return remote(
            rs.at[direction, f, p], rs.at[direction, f, p + odd],
            rs_send.at[direction, f, p], rs_recv.at[direction, f, p + odd], to,
        )

    def arrived(f, direction, p):
        remote(
            rs.at[direction, f, p], rs.at[direction, f, p],
            rs_send.at[direction, f, p], rs_recv.at[direction, f, p], partner,
        ).wait_recv()
        return rs[direction, f, p].astype(F32)

    def last_copy(f):
        return remote(
            rs.at[0, f, 2], bt.at[u % 2, f // NY], b_send.at[f], b_recv.at[u % 2, f // NY], there(row_block(f), v, z)
        )

    def product(f, root):
        rows = pl.ds(pl.multiple_of(row_block(f) * ROWS, ROWS), ROWS)
        return dot(xg[rows, :], wg[root // 2, f // NY], 1, 0)

    def in_turn(i):
        return (i >= 0) & (i < NQ * PERIOD) & (i % PERIOD < NY)

    def flow(i):
        return (i // PERIOD) * NY + i % PERIOD

    def first_direction(f):
        return f % 2

    def tile_step(i):
        @pl.when((odd == 0) & in_turn(i))
        def _():
            f4 = flow(i)
            part = product(f4, (z + 4) % NZ).astype(BF)
            for direction in range(2):
                @pl.when(first_direction(f4) == direction)
                def _():
                    rs[direction, f4, 0] = part
                    ring_copy(f4, direction, 0).start()

        i3 = i - LAGS[1]
        f3 = flow(i3)

        @pl.when((odd == 1) & in_turn(i3))
        def _():
            for direction in range(2):
                root = (z + 3) % NZ if direction == 0 else (z + NZ - 3) % NZ
                part = product(f3, root)

                @pl.when(first_direction(f3) == direction)
                def _():
                    rs[direction, f3, 0] = (part + arrived(f3, direction, 0)).astype(BF)

                @pl.when(first_direction(f3) != direction)
                def _():
                    rs[direction, f3, 0] = part.astype(BF)

                ring_copy(f3, direction, 0).start()

        away = 2 - odd
        i1 = i - LAGS[2] - odd * (LAGS[3] - LAGS[2])
        f1 = flow(i1)

        @pl.when(in_turn(i1))
        def _():
            for direction in range(2):
                root = (z + away) % NZ if direction == 0 else (z + NZ - away) % NZ
                part = product(f1, root)
                rs[direction, f1, 1] = (part + arrived(f1, direction, 1)).astype(BF)
                ring_copy(f1, direction, 1).start()

        i0 = i - LAGS[4]
        f0 = flow(i0)

        @pl.when((odd == 0) & in_turn(i0))
        def _():
            part = product(f0, z)
            part = part + arrived(f0, 0, 2)
            rs[0, f0, 2] = (part + arrived(f0, 1, 2)).astype(BF)
            last_copy(f0).start()

    def shrink_part(c):
        if c == 0:
            load_shrink.wait()
            for d in range(1, NX):
                src = (v + NX - d) % NX
                remote(ain.at[src], ain.at[src], f_send.at[d - 1], f_recv.at[d - 1], partner).wait_recv()
                remote(sin.at[src], sin.at[src], g_send.at[d - 1], g_recv.at[d - 1], partner).wait_recv()
            total[...] = jnp.zeros_like(total)

        count = SLOTS // PARTS
        projected = dot(
            shrink[pl.ds(c * (count * RANK), count * RANK), :], ain[...].reshape(NX * GROUP, WIDTH), 1, 1
        )
        for vv in range(NX):
            slots = sin[vv, 0:1, :].astype(jnp.int32) - c * count
            sums = total[vv]
            for k in range(count):
                sums = sums + jnp.where(
                    slots == k, projected[k * RANK : (k + 1) * RANK, vv * GROUP : (vv + 1) * GROUP], 0.0
                )
            total[vv] = sums

        if c == PARTS - 1:
            pin[z] = total[...].astype(BF)
            for d in range(1, NZ):
                sum_copy(d).start()

    def sum_copy(d):
        return remote(pin.at[z], pin.at[z], z_send.at[d - 1], z_recv.at[d - 1], here(u, v, (z + d) % NZ))

    def return_copy(vv, b):
        return remote(
            low.at[vv, pl.ds(b * CAP, CAP), :], lin.at[dp], r_send.at[vv, b], r_recv.at[dp], there(b, vv, z)
        )

    def expand_part(turn):
        vv = (v + (2, 1, 3, 0)[turn]) % NX
        if turn == 0:
            load_expand.wait()
            for d in range(1, NZ):
                src = (z + NZ - d) % NZ
                remote(pin.at[src], pin.at[src], z_send.at[d - 1], z_recv.at[d - 1], partner).wait_recv()

        sums = pin[0, vv].astype(F32)
        for k in range(1, NZ):
            sums = sums + pin[k, vv].astype(F32)
        slots = sin[vv, 0:1, :].astype(jnp.int32)
        for k in range(SLOTS):
            spread[k * RANK : (k + 1) * RANK, :] = jnp.where(slots == k, sums, 0.0).astype(BF)
        low[vv] = dot(spread[...], expand[...], 0, 0).astype(BF)
        for d in (2, 1, 3, 0):
            return_copy(vv, (u + d) % NY).start()

    def round_of(j, carry):
        @pl.when(in_turn(j) & (j % PERIOD == 0))
        def _():
            gw(j // PERIOD)[5]()

        for f in range(1, NY):
            pl.when(j == f)(gx[1 + f])

        for chunk, at in PASS_W.items():
            pl.when(j == at)(gw(chunk)[1])
        for chunk, at in SEND_W.items():
            pl.when(j == at)(gw(chunk)[0])

        tile_step(j)

        pl.when(j == ROUTE_AT)(route)
        for c in range(PARTS):
            pl.when(j == SHRINK_AT[c])(functools.partial(shrink_part, c))
        for vv in range(NX):
            pl.when(j == EXPAND_AT[vv])(functools.partial(expand_part, vv))
        return carry

    lax.fori_loop(0, ROUNDS, round_of, 0)

    remote(block_of(u), xp, p_send.at[0], p_recv.at[0], partner).wait_recv()
    remote(idg.at[u], idp, p_send.at[1], p_recv.at[1], partner).wait_recv()
    owner = idp[0:1, :]
    code = owner * CAP + arrivals(owner, upper)
    pick = (lax.broadcasted_iota(jnp.int32, (OWNERS * CAP, ROWS), 0) == code).astype(BF)
    for copy in started:
        copy.wait_send()
    gx[6]()
    for q in range(NQ):
        gw(q)[6]()
    for d in range(1, NX):
        route_copy(d, (v + d) % NX).wait_send()
        slot_copy(d, (v + d) % NX).wait_send()
    for d in range(1, NZ):
        sum_copy(d).wait_send()

    def drain_flow(f, carry):
        for direction in range(2):
            pl.when((odd == 1) | (first_direction(f) == direction))(
                lambda: ring_copy(f, direction, 0).wait_send()
            )
            ring_copy(f, direction, 1).wait_send()
        pl.when(odd == 0)(lambda: last_copy(f).wait_send())
        return carry

    lax.fori_loop(0, FLOWS - NY, drain_flow, 0)

    for o in range(OWNERS):
        remote(lin.at[o], lin.at[o], r_send.at[0, 0], r_recv.at[o], partner).wait_recv()
    for c in range(WIDTH // 256):
        cols = slice(c * 256, (c + 1) * 256)
        rows = dot(pick, lin[:, :, cols].reshape(OWNERS * CAP, 256), 0, 0)
        acc[:, cols] = xp[:, cols].astype(F32) + rows
    for vv in range(NX):
        for b in range(NY):
            return_copy(vv, b).wait_send()
    for q in range(NQ):
        for p in range(2):
            remote(bt.at[p, q], bt.at[p, q], b_send.at[q], b_recv.at[p, q], partner).wait_recv()
            cols = slice(p * COLS + q * CW, p * COLS + (q + 1) * CW)
            out_ref[:, cols] = (acc[:, cols] + bt[p, q].astype(F32)).astype(BF)
    lax.fori_loop(FLOWS - NY, FLOWS, drain_flow, 0)


def local_part(hidden_states, base_weight, shrink_weight, expand_weight, owner_ids, adapter_slots):
    ids = jnp.concatenate(
        [owner_ids.reshape(1, ROWS), adapter_slots.reshape(1, ROWS), jnp.zeros((6, ROWS), jnp.int32)], axis=0
    )
    dma = pltpu.SemaphoreType.DMA
    any_spec = pl.BlockSpec(memory_space=pl.ANY)
    out = pl.pallas_call(
        kernel,
        out_shape=jax.ShapeDtypeStruct((ROWS, WIDTH), BF),
        in_specs=[any_spec] * 5,
        out_specs=pl.BlockSpec(memory_space=pltpu.VMEM),
        scratch_shapes=[
            pltpu.VMEM((NY * ROWS, WIDTH), BF),
            pltpu.VMEM((NX, NQ, WIDTH, CW), BF),
            pltpu.VMEM((NY, 8, ROWS), jnp.int32),
            pltpu.VMEM((2, FLOWS, STEPS, ROWS, CW), BF),
            pltpu.VMEM((2, NQ, ROWS, CW), BF),
            pltpu.VMEM((ROWS, WIDTH), BF),
            pltpu.VMEM((8, ROWS), jnp.int32),
            pltpu.VMEM((NX, GROUP, WIDTH), BF),
            pltpu.VMEM((NX, 8, GROUP), F32),
            pltpu.VMEM((NX, GROUP, WIDTH), BF),
            pltpu.VMEM((NX, 8, GROUP), F32),
            pltpu.VMEM((SLOTS * RANK, WIDTH), BF),
            pltpu.VMEM((SLOTS * RANK, WIDTH), BF),
            pltpu.VMEM((NX, RANK, GROUP), F32),
            pltpu.VMEM((NZ, NX, RANK, GROUP), BF),
            pltpu.VMEM((SLOTS * RANK, GROUP), BF),
            pltpu.VMEM((NX, GROUP, WIDTH), BF),
            pltpu.VMEM((OWNERS, CAP, WIDTH), BF),
            pltpu.VMEM((ROWS, WIDTH), F32),
            dma((4 + NQ,)),
            dma((6,)), dma((6,)),
            dma((NY - 1,)), dma((NY - 1,)),
            dma((NQ, 6)), dma((NQ, 6)),
            dma((2,)), dma((2,)),
            dma((NX - 1,)), dma((NX - 1,)),
            dma((NX - 1,)), dma((NX - 1,)),
            dma((NZ - 1,)), dma((NZ - 1,)),
            dma((NX, NY)), dma((OWNERS,)),
            dma((FLOWS,)), dma((2, NQ)),
            dma((2, FLOWS, STEPS)), dma((2, FLOWS, STEPS)),
        ],
        compiler_params=pltpu.CompilerParams(
            collective_id=0, has_side_effects=True, vmem_limit_bytes=56 << 20
        ),
    )(
        hidden_states[0],
        base_weight[0],
        shrink_weight[0].reshape(SLOTS * RANK, WIDTH),
        expand_weight[0].reshape(SLOTS * RANK, WIDTH),
        ids,
    )
    return out[None]


def solution(mesh):
    return jax.shard_map(
        local_part,
        mesh=mesh,
        in_specs=(
            P("section", "dp", "tensor"),
            P("section", "tensor", "dp"),
            P("section", "dp", None, "tensor"),
            P("section", "dp", None, "tensor"),
            P("section", "dp", None),
            P("section", "dp"),
        ),
        out_specs=P("section", "dp", "tensor"),
        check_vma=False,
    )
```

```python
import functools

import jax
import jax.numpy as jnp
from jax import lax
from jax.experimental import pallas as pl
from jax.experimental.pallas import tpu as pltpu
from jax.sharding import PartitionSpec as P

MESH = pl.DeviceIdType.MESH
NX, NY, NZ = 4, 4, 8
ROWS, WIDTH, COLS = 256, 1024, 512
OWNERS, CAP, SLOTS, RANK = 16, 32, 64, 16
NQ = 4
CW = COLS // NQ
GROUP = NY * CAP
FLOWS = NQ * NY
STEPS = 3
GAP = 1
PERIOD = NY + GAP
LAGS = (0, 2, 4, 6, 8)
ROUNDS = NQ * PERIOD - GAP + LAGS[4]
SEND_W = {2: 1, 3: 6}
PASS_W = {1: 1, 2: 6, 3: 11}
ROUTE_AT = 11
SHRINK_AT = (17, 17, 18, 18)
EXPAND_AT = (20, 21, 22, 23)
PARTS = 4
BF, F32 = jnp.bfloat16, jnp.float32


def remote(src, dst, send, recv, device):
    return pltpu.make_async_remote_copy(
        src_ref=src, dst_ref=dst, send_sem=send, recv_sem=recv, device_id=device, device_id_type=MESH
    )


def dot(a, b, ca, cb):
    return lax.dot_general(a, b, (((ca,), (cb,)), ((), ())), preferred_element_type=F32)


def arrivals(owner, upper):
    hits = lax.broadcasted_iota(jnp.int32, (OWNERS, ROWS), 0) == owner
    count = dot(hits.astype(BF), upper, 1, 0)
    return (jnp.sum(jnp.where(hits, count, 0.0), axis=0, keepdims=True) - 1.0).astype(jnp.int32)


def kernel(
    x_hbm, w_hbm, shrink_hbm, expand_hbm, ids_hbm, out_ref,
    xg, wg, idg, rs, bt, xp, idp, aout, sout, ain, sin, shrink, expand, total, pin, spread, low, lin, acc,
    loc_sem, x_send, x_recv, id_send, id_recv, w_send, w_recv, p_send, p_recv, f_send, f_recv,
    g_send, g_recv, z_send, z_recv, r_send, r_recv, b_send, b_recv, rs_send, rs_recv,
):
    s = lax.axis_index("section")
    dp = lax.axis_index("dp")
    z = lax.axis_index("tensor")
    x, y = dp // NY, dp % NY
    u, v = y, x
    place = lambda uu, vv: vv * NY + uu
    here = lambda uu, vv, zz: (s, place(uu, vv), zz)
    there = lambda uu, vv, zz: (1 - s, place(uu, vv), zz)
    odd = (z + u // 2) % 2
    partner = (1 - s, dp, z)

    def local(src, dst, i):
        return pltpu.make_async_copy(src, dst, loc_sem.at[i])

    block_of = lambda b: xg.at[pl.ds(pl.multiple_of(b * ROWS, ROWS), ROWS), :]
    load_x = local(x_hbm, block_of(u), 0)
    load_id = local(ids_hbm, idg.at[u], 1)
    load_w = [local(w_hbm.at[:, pl.ds(q * CW, CW)], wg.at[v, q], 4 + q) for q in range(NQ)]
    load_shrink = local(shrink_hbm, shrink, 2)
    load_expand = local(expand_hbm, expand, 3)
    load_x.start()
    for q in range(NQ):
        load_w[q].start()
    load_id.start()

    barrier = pltpu.get_barrier_semaphore()
    peers = [here((u + d) % NY, v, z) for d in range(1, NY)]
    peers += [here(u, (v + d) % NX, z) for d in range(1, NX)]
    peers += [here(u, v, (z + d) % NZ) for d in range(1, NZ)]
    peers += [(1 - s, o, z) for o in range(OWNERS)]
    for peer in peers:
        pl.semaphore_signal(barrier, inc=1, device_id=peer, device_id_type=MESH)
    pl.semaphore_wait(barrier, len(peers))

    started = []

    def start(copy):
        copy.start()
        started.append(copy)

    def gather(buf, slots, send, recv, up, down):
        mine, below, above, far = slots
        sends = [remote(buf(mine, h), buf(mine, h), send(i), recv(i), to) for i, (h, to) in enumerate(
            [(0, up), (1, down), (1, up), (0, down)])]
        arrive = [remote(buf(slot, h), buf(slot, h), send(i), recv(i), up) for i, (slot, h) in enumerate(
            [(below, 0), (above, 1), (below, 1), (above, 0)])]
        pass_up = remote(buf(below, 0), buf(below, 0), send(4), recv(4), up)
        pass_down = remote(buf(above, 1), buf(above, 1), send(5), recv(5), down)
        far_up = remote(buf(far, 0), buf(far, 0), send(4), recv(4), up)
        far_down = remote(buf(far, 1), buf(far, 1), send(5), recv(5), down)

        def first():
            for copy in sends:
                copy.start()

        def forward():
            arrive[0].wait_recv()
            pass_up.start()
            arrive[1].wait_recv()
            pass_down.start()

        def finish_below():
            arrive[2].wait_recv()

        def finish_above():
            arrive[3].wait_recv()

        def finish_far():
            far_up.wait_recv()
            far_down.wait_recv()

        def finish():
            finish_below()
            finish_above()
            finish_far()

        def drain():
            for copy in sends:
                copy.wait_send()
            pass_up.wait_send()
            pass_down.wait_send()

        return first, forward, finish_below, finish_above, finish_far, finish, drain

    u_up, u_down, u_far = (u + 1) % NY, (u + NY - 1) % NY, (u + 2) % NY
    v_up, v_down, v_far = (v + 1) % NX, (v + NX - 1) % NX, (v + 2) % NX
    x_buf = lambda slot, h: xg.at[pl.ds(pl.multiple_of(slot * ROWS + h * (ROWS // 2), ROWS // 2), ROWS // 2), :]
    w_buf = lambda q: lambda slot, h: wg.at[slot, q, pl.ds(h * (WIDTH // 2), WIDTH // 2), :]
    gx = gather(
        x_buf, (u, u_down, u_up, u_far), lambda i: x_send.at[i], lambda i: x_recv.at[i],
        here(u_up, v, z), here(u_down, v, z),
    )
    gw = lambda q: gather(
        w_buf(q), (v, v_down, v_up, v_far), lambda i: w_send.at[q, i], lambda i: w_recv.at[q, i],
        here(u, v_up, z), here(u, v_down, z),
    )

    load_x.wait()
    gx[0]()
    load_w[0].wait()
    gw(0)[0]()
    load_id.wait()
    for d in range(1, NY):
        start(remote(idg.at[u], idg.at[u], id_send.at[d - 1], id_recv.at[d - 1], here((u + d) % NY, v, z)))

    load_shrink.start()
    load_expand.start()
    for q in range(1, NQ):
        load_w[q].wait()
    gw(0)[1]()
    gw(1)[0]()
    gx[1]()
    start(remote(block_of(u), xp, p_send.at[0], p_recv.at[0], partner))
    start(remote(idg.at[u], idp, p_send.at[1], p_recv.at[1], partner))

    upper = (
        lax.broadcasted_iota(jnp.int32, (ROWS, ROWS), 0) <= lax.broadcasted_iota(jnp.int32, (ROWS, ROWS), 1)
    ).astype(BF)

    def route():
        for d in range(1, NY):
            src = (u + NY - d) % NY
            remote(idg.at[src], idg.at[src], id_send.at[d - 1], id_recv.at[d - 1], partner).wait_recv()
        for b in range(NY):
            owner = idg[b, 0:1, :]
            code = jnp.where((owner & 3) == u, (owner >> 2) * CAP + arrivals(owner, upper), -1)
            pick = (lax.broadcasted_iota(jnp.int32, (NX * CAP, ROWS), 0) == code).astype(BF)
            rows = dot(pick, xg[b * ROWS : (b + 1) * ROWS, :], 1, 0).astype(BF)
            for vv in range(NX):
                aout[vv, b * CAP : (b + 1) * CAP, :] = rows[vv * CAP : (vv + 1) * CAP]
            place_in = (
                lax.broadcasted_iota(jnp.int32, (NX * GROUP, ROWS), 0)
                == jnp.where(code < 0, -1, (code >> 5) * GROUP + b * CAP + (code & 31))
            ).astype(BF)
            slot_block = jnp.broadcast_to(idg[b, 1:2, :].astype(F32).astype(BF), (8, ROWS))
            chosen = dot(slot_block, place_in, 1, 1)
            for vv in range(NX):
                part = chosen[:, vv * GROUP : (vv + 1) * GROUP]
                sout[vv] = part if b == 0 else sout[vv] + part
        for d in (2, 1, 3):
            to = (v + d) % NX
            route_copy(d, to).start()
            slot_copy(d, to).start()
        ain[v] = aout[v]
        sin[v] = sout[v]

    def route_copy(d, to):
        return remote(aout.at[to], ain.at[v], f_send.at[d - 1], f_recv.at[d - 1], here(u, to, z))

    def slot_copy(d, to):
        return remote(sout.at[to], sin.at[v], g_send.at[d - 1], g_recv.at[d - 1], here(u, to, z))

    def row_block(f):
        r = f % NY
        return (u + ((r + 3) // 4) * ((r + 1) % 3 + 1)) % NY

    def ring_copy(f, direction, p):
        to = here(u, v, (z + 1) % NZ if direction == 0 else (z + NZ - 1) % NZ)
        return remote(
            rs.at[direction, f, p], rs.at[direction, f, p + odd],
            rs_send.at[direction, f, p], rs_recv.at[direction, f, p + odd], to,
        )

    def arrived(f, direction, p):
        remote(
            rs.at[direction, f, p], rs.at[direction, f, p],
            rs_send.at[direction, f, p], rs_recv.at[direction, f, p], partner,
        ).wait_recv()
        return rs[direction, f, p].astype(F32)

    def last_copy(f):
        return remote(
            rs.at[0, f, 2], bt.at[u % 2, f // NY], b_send.at[f], b_recv.at[u % 2, f // NY], there(row_block(f), v, z)
        )

    def product(f, root):
        rows = pl.ds(pl.multiple_of(row_block(f) * ROWS, ROWS), ROWS)
        return dot(xg[rows, :], wg[root // 2, f // NY], 1, 0)

    def in_turn(i):
        return (i >= 0) & (i < NQ * PERIOD) & (i % PERIOD < NY)

    def flow(i):
        return (i // PERIOD) * NY + i % PERIOD

    def first_direction(f):
        return f % 2

    def tile_step(i):
        @pl.when((odd == 0) & in_turn(i))
        def _():
            f4 = flow(i)
            part = product(f4, (z + 4) % NZ).astype(BF)
            for direction in range(2):
                @pl.when(first_direction(f4) == direction)
                def _():
                    rs[direction, f4, 0] = part
                    ring_copy(f4, direction, 0).start()

        i3 = i - LAGS[1]
        f3 = flow(i3)

        @pl.when((odd == 1) & in_turn(i3))
        def _():
            for direction in range(2):
                root = (z + 3) % NZ if direction == 0 else (z + NZ - 3) % NZ
                part = product(f3, root)

                @pl.when(first_direction(f3) == direction)
                def _():
                    rs[direction, f3, 0] = (part + arrived(f3, direction, 0)).astype(BF)

                @pl.when(first_direction(f3) != direction)
                def _():
                    rs[direction, f3, 0] = part.astype(BF)

                ring_copy(f3, direction, 0).start()

        away = 2 - odd
        i1 = i - LAGS[2] - odd * (LAGS[3] - LAGS[2])
        f1 = flow(i1)

        @pl.when(in_turn(i1))
        def _():
            for direction in range(2):
                root = (z + away) % NZ if direction == 0 else (z + NZ - away) % NZ
                part = product(f1, root)
                rs[direction, f1, 1] = (part + arrived(f1, direction, 1)).astype(BF)
                ring_copy(f1, direction, 1).start()

        i0 = i - LAGS[4]
        f0 = flow(i0)

        @pl.when((odd == 0) & in_turn(i0))
        def _():
            part = product(f0, z)
            part = part + arrived(f0, 0, 2)
            rs[0, f0, 2] = (part + arrived(f0, 1, 2)).astype(BF)
            last_copy(f0).start()

    def shrink_part(c):
        if c == 0:
            load_shrink.wait()
            for d in range(1, NX):
                src = (v + NX - d) % NX
                remote(ain.at[src], ain.at[src], f_send.at[d - 1], f_recv.at[d - 1], partner).wait_recv()
                remote(sin.at[src], sin.at[src], g_send.at[d - 1], g_recv.at[d - 1], partner).wait_recv()
            total[...] = jnp.zeros_like(total)

        count = SLOTS // PARTS
        projected = dot(
            shrink[pl.ds(c * (count * RANK), count * RANK), :], ain[...].reshape(NX * GROUP, WIDTH), 1, 1
        )
        for vv in range(NX):
            slots = sin[vv, 0:1, :].astype(jnp.int32) - c * count
            sums = total[vv]
            for k in range(count):
                sums = sums + jnp.where(
                    slots == k, projected[k * RANK : (k + 1) * RANK, vv * GROUP : (vv + 1) * GROUP], 0.0
                )
            total[vv] = sums

        if c == PARTS - 1:
            pin[z] = total[...].astype(BF)
            for d in (4, 3, 5, 2, 6, 1, 7):
                sum_copy(d).start()

    def sum_copy(d):
        return remote(pin.at[z], pin.at[z], z_send.at[d - 1], z_recv.at[d - 1], here(u, v, (z + d) % NZ))

    def return_copy(vv, b):
        return remote(
            low.at[vv, pl.ds(b * CAP, CAP), :], lin.at[dp], r_send.at[vv, b], r_recv.at[dp], there(b, vv, z)
        )

    def expand_part(turn):
        vv = (v + (2, 1, 3, 0)[turn]) % NX
        if turn == 0:
            load_expand.wait()
            for d in range(1, NZ):
                src = (z + NZ - d) % NZ
                remote(pin.at[src], pin.at[src], z_send.at[d - 1], z_recv.at[d - 1], partner).wait_recv()

        sums = pin[0, vv].astype(F32)
        for k in range(1, NZ):
            sums = sums + pin[k, vv].astype(F32)
        slots = sin[vv, 0:1, :].astype(jnp.int32)
        for k in range(SLOTS):
            spread[k * RANK : (k + 1) * RANK, :] = jnp.where(slots == k, sums, 0.0).astype(BF)
        low[vv] = dot(spread[...], expand[...], 0, 0).astype(BF)
        for d in (2, 1, 3, 0):
            return_copy(vv, (u + d) % NY).start()

    def round_of(j, carry):
        @pl.when(in_turn(j) & (j % PERIOD == 0))
        def _():
            gw(j // PERIOD)[5]()

        for f in range(1, NY):
            pl.when(j == f)(gx[1 + f])

        for chunk, at in PASS_W.items():
            pl.when(j == at)(gw(chunk)[1])
        for chunk, at in SEND_W.items():
            pl.when(j == at)(gw(chunk)[0])

        tile_step(j)

        pl.when(j == ROUTE_AT)(route)
        for c in range(PARTS):
            pl.when(j == SHRINK_AT[c])(functools.partial(shrink_part, c))
        for vv in range(NX):
            pl.when(j == EXPAND_AT[vv])(functools.partial(expand_part, vv))
        return carry

    lax.fori_loop(0, ROUNDS, round_of, 0)

    remote(block_of(u), xp, p_send.at[0], p_recv.at[0], partner).wait_recv()
    remote(idg.at[u], idp, p_send.at[1], p_recv.at[1], partner).wait_recv()
    owner = idp[0:1, :]
    code = owner * CAP + arrivals(owner, upper)
    pick = (lax.broadcasted_iota(jnp.int32, (OWNERS * CAP, ROWS), 0) == code).astype(BF)
    for copy in started:
        copy.wait_send()
    gx[6]()
    for q in range(NQ):
        gw(q)[6]()
    for d in range(1, NX):
        route_copy(d, (v + d) % NX).wait_send()
        slot_copy(d, (v + d) % NX).wait_send()
    for d in range(1, NZ):
        sum_copy(d).wait_send()

    def drain_flow(f, carry):
        for direction in range(2):
            pl.when((odd == 1) | (first_direction(f) == direction))(
                lambda: ring_copy(f, direction, 0).wait_send()
            )
            ring_copy(f, direction, 1).wait_send()
        pl.when(odd == 0)(lambda: last_copy(f).wait_send())
        return carry

    lax.fori_loop(0, FLOWS - NY, drain_flow, 0)

    for o in range(OWNERS):
        remote(lin.at[o], lin.at[o], r_send.at[0, 0], r_recv.at[o], partner).wait_recv()
    for c in range(WIDTH // 256):
        cols = slice(c * 256, (c + 1) * 256)
        rows = dot(pick, lin[:, :, cols].reshape(OWNERS * CAP, 256), 0, 0)
        acc[:, cols] = xp[:, cols].astype(F32) + rows
    for vv in range(NX):
        for b in range(NY):
            return_copy(vv, b).wait_send()
    for q in range(NQ):
        for p in range(2):
            remote(bt.at[p, q], bt.at[p, q], b_send.at[q], b_recv.at[p, q], partner).wait_recv()
            cols = slice(p * COLS + q * CW, p * COLS + (q + 1) * CW)
            out_ref[:, cols] = (acc[:, cols] + bt[p, q].astype(F32)).astype(BF)
    lax.fori_loop(FLOWS - NY, FLOWS, drain_flow, 0)


def local_part(hidden_states, base_weight, shrink_weight, expand_weight, owner_ids, adapter_slots):
    ids = jnp.concatenate(
        [owner_ids.reshape(1, ROWS), adapter_slots.reshape(1, ROWS), jnp.zeros((6, ROWS), jnp.int32)], axis=0
    )
    dma = pltpu.SemaphoreType.DMA
    any_spec = pl.BlockSpec(memory_space=pl.ANY)
    out = pl.pallas_call(
        kernel,
        out_shape=jax.ShapeDtypeStruct((ROWS, WIDTH), BF),
        in_specs=[any_spec] * 5,
        out_specs=pl.BlockSpec(memory_space=pltpu.VMEM),
        scratch_shapes=[
            pltpu.VMEM((NY * ROWS, WIDTH), BF),
            pltpu.VMEM((NX, NQ, WIDTH, CW), BF),
            pltpu.VMEM((NY, 8, ROWS), jnp.int32),
            pltpu.VMEM((2, FLOWS, STEPS, ROWS, CW), BF),
            pltpu.VMEM((2, NQ, ROWS, CW), BF),
            pltpu.VMEM((ROWS, WIDTH), BF),
            pltpu.VMEM((8, ROWS), jnp.int32),
            pltpu.VMEM((NX, GROUP, WIDTH), BF),
            pltpu.VMEM((NX, 8, GROUP), F32),
            pltpu.VMEM((NX, GROUP, WIDTH), BF),
            pltpu.VMEM((NX, 8, GROUP), F32),
            pltpu.VMEM((SLOTS * RANK, WIDTH), BF),
            pltpu.VMEM((SLOTS * RANK, WIDTH), BF),
            pltpu.VMEM((NX, RANK, GROUP), F32),
            pltpu.VMEM((NZ, NX, RANK, GROUP), BF),
            pltpu.VMEM((SLOTS * RANK, GROUP), BF),
            pltpu.VMEM((NX, GROUP, WIDTH), BF),
            pltpu.VMEM((OWNERS, CAP, WIDTH), BF),
            pltpu.VMEM((ROWS, WIDTH), F32),
            dma((4 + NQ,)),
            dma((6,)), dma((6,)),
            dma((NY - 1,)), dma((NY - 1,)),
            dma((NQ, 6)), dma((NQ, 6)),
            dma((2,)), dma((2,)),
            dma((NX - 1,)), dma((NX - 1,)),
            dma((NX - 1,)), dma((NX - 1,)),
            dma((NZ - 1,)), dma((NZ - 1,)),
            dma((NX, NY)), dma((OWNERS,)),
            dma((FLOWS,)), dma((2, NQ)),
            dma((2, FLOWS, STEPS)), dma((2, FLOWS, STEPS)),
        ],
        compiler_params=pltpu.CompilerParams(
            collective_id=0, has_side_effects=True, vmem_limit_bytes=56 << 20
        ),
    )(
        hidden_states[0],
        base_weight[0],
        shrink_weight[0].reshape(SLOTS * RANK, WIDTH),
        expand_weight[0].reshape(SLOTS * RANK, WIDTH),
        ids,
    )
    return out[None]


def solution(mesh):
    return jax.shard_map(
        local_part,
        mesh=mesh,
        in_specs=(
            P("section", "dp", "tensor"),
            P("section", "tensor", "dp"),
            P("section", "dp", None, "tensor"),
            P("section", "dp", None, "tensor"),
            P("section", "dp", None),
            P("section", "dp"),
        ),
        out_specs=P("section", "dp", "tensor"),
        check_vma=False,
    )
```
